512 devices in a mesh: region: 128 (over z, y, core), coarse: 4 (over x).
Axes of the slice: x: 4, y: 4, z: 16, core: 2. Of those that a mesh axis runs over, the one named last changes fastest.
Arguments:
- source_jump: float32 [512, 768, 256], P(('region', 'coarse')), may hold values from -6 to 6
- neumann_inverse: bfloat16 [512, 768, 768], P(('region', 'coarse')), may hold values from -1 to 2, as said below
- dirichlet_schur: bfloat16 [512, 768, 768], P(('region', 'coarse')), may hold values from -10 to 20, as said below
- corner_coupling: float32 [512, 4, 768], P(('region', 'coarse')), may hold values from -0.21875 to 0.21875
- corner_map: int32 [512, 4], P(('region', 'coarse')), may hold values from 0 to 515, as said below
- face_map: int32 [512, 2, 192], P(('region', 'coarse')), may hold values from 0 to 191, each once within a row
- coarse_inverse: float32 [516, 516], P('coarse'), may hold values from -1 to 2, as said below
Outputs:
- multiplier: float32 [512, 768, 256], P(('region', 'coarse'))
- residual: float32 [512, 768, 256], P(('region', 'coarse'))
The draws below stay inside these ranges and needn't reach their ends.
Inputs may be any that keep to these rules, and one draw needn't show every extreme that they name: `corner_map`: subdomain (a, b) names, in an order of its own, the coarse unknowns of the four grid vertices (a or a+1, b or b+1 mod 4) that its vertical edges stand on; the unknowns of vertices (a', 0) to (a', 4 - 1) are a' 4 to a' 4 + 4 - 1 in some order. `face_map`: each row of each face is a permutation. `neumann_inverse`: each subdomain's matrix is symmetric positive definite. `dirichlet_schur`: each subdomain's matrix is symmetric positive definite. `coarse_inverse`: symmetric positive definite.
All inputs are finite; a program needn't handle non-finite values.
Results may differ from the reference program's by a relative error of at most 0.0051.
Values sent between devices are 32-bit elements; how exact they have to be, the bound alone decides.
A program may use at most 64 MiB of HBM per device.

```python
import math
import jax
import jax.numpy as jnp
from jax import lax

M = 768
FACE = 192
NC = 4
K = 256
ITERS = 3
NSUB = 512
NCOARSE = 516
N_REGION = 128
N_COARSE = 4


def conductivity(key):
    return jnp.exp(jax.random.uniform(key, (NSUB,), jnp.float32, 0.0, math.log(10.0)))


def coupled(key, order, factor):
    first_key, second_key = jax.random.split(key)
    diagonal = jax.random.uniform(first_key, (order,), jnp.float32, 1.0, 2.0)
    factors = jax.random.randint(second_key, (order, order // 2), -2, 3).astype(jnp.float32)
    outer_sum = jnp.dot(factors, factors.T, precision=lax.Precision.HIGHEST)
    places = jnp.arange(order)
    leading = jnp.where(places[:, None] == places[None, :], diagonal[:, None], 0.0)
    return factor * 0.5 * (leading + outer_sum / order)


def draw_neumann_inverse(key, part):
    scales = conductivity(key)
    key = jax.random.fold_in(key, 11)

    def single(subdomain):
        return coupled(jax.random.fold_in(key, subdomain), M, 1.0 / scales[subdomain]).astype(jnp.bfloat16)
    return lax.map(single, jnp.arange(NSUB))


def draw_dirichlet_schur(key, part):
    scales = conductivity(key)
    key = jax.random.fold_in(key, 12)

    def single(subdomain):
        return coupled(jax.random.fold_in(key, subdomain), M, scales[subdomain]).astype(jnp.bfloat16)
    return lax.map(single, jnp.arange(NSUB))


def draw_coarse_inverse(key, part):
    key = jax.random.fold_in(key, 13)
    return coupled(key, NCOARSE, 1.0)


def draw_corner_map(key, part):
    key = jax.random.fold_in(key, 21)
    label_key, order_key = jax.random.split(key)
    relabel = jax.vmap(lambda single_key: jax.random.permutation(single_key, N_COARSE))(jax.random.split(label_key, N_REGION + 1)).astype(jnp.int32)
    places = jnp.arange(NSUB, dtype=jnp.int32)
    region_place = places // N_COARSE
    coarse_place = places % N_COARSE
    following = (coarse_place + 1) % N_COARSE
    vertex_rows = jnp.stack([region_place, region_place, region_place + 1, region_place + 1], axis=1)
    vertex_cols = jnp.stack([coarse_place, following, coarse_place, following], axis=1)
    numbers = vertex_rows * N_COARSE + relabel[vertex_rows, vertex_cols]
    shuffle = jax.vmap(lambda single_key: jax.random.permutation(single_key, NC))(jax.random.split(order_key, NSUB)).astype(jnp.int32)
    return jnp.take_along_axis(numbers, shuffle, axis=1).astype(jnp.int32)


def steps_of(rng, extent, pieces, low, largest):
    gain = 1.0
    for dim, blocks in pieces:
        draws = jax.random.uniform(jax.random.fold_in(jax.random.fold_in(rng, 6), dim), (blocks,), jnp.float32, low / len(pieces), largest / len(pieces))
        gain = gain * jnp.repeat(jnp.exp(draws), extent[dim] // blocks).reshape((-1,) + (1,) * (len(extent) - 1 - dim))
    return gain


def gaussian(key, dims, deviation, reach, cuts=(), kind=jnp.bfloat16):
    gain = steps_of(key, dims, cuts, -0.22, 0.18) if cuts else 1.0
    values = jax.random.normal(key, dims, jnp.float32) * deviation * gain
    return jnp.minimum(jnp.maximum(values, -reach), reach).astype(kind)


def setup_inputs(seed: int = 0) -> dict:
    arg_keys = jax.random.split(jax.random.key(seed), 8)
    source_jump = gaussian(arg_keys[0], (NSUB, M, K), 1.0, 6.0, ((0, 512),), jnp.float32)
    neumann_inverse = draw_neumann_inverse(jax.random.fold_in(arg_keys[7], 71), 0)
    dirichlet_schur = draw_dirichlet_schur(jax.random.fold_in(arg_keys[7], 71), 0)
    corner_coupling = gaussian(arg_keys[3], (NSUB, NC, M), M ** -0.5, 0.21875, ((0, 512),), jnp.float32)
    corner_map = draw_corner_map(jax.random.fold_in(arg_keys[7], 71), 0)
    face_map = jax.vmap(lambda own: jax.random.permutation(own, FACE))(jax.random.split(arg_keys[5], NSUB * 2)).reshape((NSUB, 2, FACE)).astype(jnp.int32)
    coarse_inverse = draw_coarse_inverse(jax.random.fold_in(arg_keys[7], 71), 0)
    return {"source_jump": source_jump, "neumann_inverse": neumann_inverse, "dirichlet_schur": dirichlet_schur, "corner_coupling": corner_coupling, "corner_map": corner_map, "face_map": face_map, "coarse_inverse": coarse_inverse}


def pick_rows(values, order):
    return jnp.take_along_axis(values, order[..., None], axis=2)


def dual_jump(field, face_map):
    faces = field.reshape(N_REGION, N_COARSE, 4, FACE, K)
    forward_region = face_map[:, 0].reshape(N_REGION, N_COARSE, FACE)
    forward_coarse = face_map[:, 1].reshape(N_REGION, N_COARSE, FACE)
    backward_region = jnp.argsort(forward_region, axis=2).astype(jnp.int32)
    backward_coarse = jnp.argsort(forward_coarse, axis=2).astype(jnp.int32)
    blank = jnp.zeros((1, N_COARSE, FACE, K), field.dtype)
    sent_region = pick_rows(faces[:, :, 1], backward_region)
    from_left = jnp.concatenate([blank, sent_region[:-1]], axis=0)
    right_faces = jnp.concatenate([faces[1:, :, 0], blank], axis=0)
    first = faces[:, :, 0] - from_left
    second = faces[:, :, 1] - pick_rows(right_faces, forward_region)
    sent_coarse = pick_rows(faces[:, :, 3], backward_coarse)
    third = faces[:, :, 2] - jnp.roll(sent_coarse, 1, axis=1)
    fourth = faces[:, :, 3] - pick_rows(jnp.roll(faces[:, :, 2], -1, axis=1), forward_coarse)
    region_place = jnp.arange(N_REGION)[:, None, None, None]
    first = jnp.where(region_place > 0, first, 0.0)
    second = jnp.where(region_place < N_REGION - 1, second, 0.0)
    return jnp.stack([first, second, third, fourth], axis=2).reshape(field.shape)


def batched_dot(matrices, vectors):
    return lax.map(lambda operands: jnp.dot(operands[0], operands[1], preferred_element_type=jnp.float32), (matrices, vectors))


def neumann_apply(direction, neumann_inverse, corner_coupling, corner_map, coarse_inverse, face_map):
    local = batched_dot(neumann_inverse, direction.astype(jnp.bfloat16))
    corner_load = jnp.einsum('scm,smk->sck', corner_coupling, direction, precision=lax.Precision.HIGHEST)
    totals = jax.ops.segment_sum(corner_load.reshape(-1, K), corner_map.reshape(-1), num_segments=NCOARSE)
    values = jnp.dot(coarse_inverse, totals, precision=lax.Precision.HIGHEST)
    corner_values = values[corner_map]
    field = local + jnp.einsum('scm,sck->smk', corner_coupling, corner_values, precision=lax.Precision.HIGHEST)
    return dual_jump(field, face_map)


def precond_apply(residual, dirichlet_schur, face_map):
    weighted = batched_dot(dirichlet_schur, (0.5 * residual).astype(jnp.bfloat16))
    return 0.5 * dual_jump(weighted, face_map)


def reference(source_jump, neumann_inverse, dirichlet_schur, corner_coupling, corner_map, face_map, coarse_inverse):
    residual = dual_jump(source_jump, face_map)
    multiplier = jnp.zeros_like(residual)
    precond = precond_apply(residual, dirichlet_schur, face_map)
    precond_sum = jnp.sum(residual * precond, axis=(0, 1))
    direction = precond
    for iteration in range(ITERS):
        image = neumann_apply(direction, neumann_inverse, corner_coupling, corner_map, coarse_inverse, face_map)
        curve_sum = jnp.sum(direction * image, axis=(0, 1))
        step_len = precond_sum / curve_sum
        multiplier = multiplier + step_len * direction
        residual = residual - step_len * image
        if iteration + 1 < ITERS:
            precond = precond_apply(residual, dirichlet_schur, face_map)
            next_sum = jnp.sum(residual * precond, axis=(0, 1))
            direction = precond + (next_sum / precond_sum) * direction
            precond_sum = next_sum
    return multiplier, residual
```

```python
import functools

import jax
import jax.numpy as jnp
from jax import lax
from jax.experimental import pallas as pl
from jax.experimental.pallas import tpu as pltpu
from jax.sharding import PartitionSpec as P

ITERS = 3
MESH = pl.DeviceIdType.MESH
F32, BF16 = jnp.float32, jnp.bfloat16

PLANE = 8
NX = 4
GROUP = PLANE * NX
NZ = 16
FACE = 192
M = 4 * FACE
K = 256
BASE = NX * PLANE
USED = NX * (PLANE + 3)
WIDE = 640


def rounded(value):
    return value.astype(BF16).astype(F32)


def dot(a, b):
    return jnp.dot(a, b, preferred_element_type=F32)


def dot_nt(a, b):
    return lax.dot_general(a, b, (((1,), (1,)), ((), ())), preferred_element_type=F32)


def permuted(onehot, value):
    high = value.astype(BF16)
    rest = value - high.astype(F32)
    middle = rest.astype(BF16)
    low = (rest - middle.astype(F32)).astype(BF16)
    return (dot(onehot, high) + dot(onehot, middle)) + dot(onehot, low)


def kernel(
    source, neumann, dirichlet, coupling, corner_map, face_map, coarse_inverse,
    x_out, r_out,
    residual, solved, search, image, weighted, dual, local,
    weighted_in, local_in, corner_out, corner_in, frame,
    perms, dirichlet_all, neumann_own, raw_dirichlet, raw_neumann, spread,
    blocks, assembled, inverse_high, inverse_low, shifted, scalars,
    loads_out, loads_in, plane_loads, all_loads, dots_out, all_dots, back_out, back_in,
    fetch_sem, face_send, source_recv, weighted_recv, local_recv, corner_send, corner_recv,
    block_send, block_recv, core_send, core_recv,
    group_send, loads_recv, plane_send, all_recv, dots_send, dots_recv, back_send, back_recv,
):
    region, coarse = lax.axis_index("region"), lax.axis_index("coarse")
    z, place = lax.div(region, PLANE), lax.rem(region, PLANE)
    core = lax.rem(region, 2)
    own = place * NX + coarse
    n_region = NZ * PLANE
    left = (lax.rem(region + n_region - 1, n_region), coarse)
    right = (lax.rem(region + 1, n_region), coarse)
    before = (region, lax.rem(coarse + NX - 1, NX))
    after = (region, lax.rem(coarse + 1, NX))
    neighbours = (left, right, before, after)
    partner_face = (1, 0, 3, 2)
    paired = (region > 0, region < n_region - 1, None, None)

    def in_group(step):
        peer = lax.rem(own + step, GROUP)
        return peer, (z * PLANE + lax.div(peer, NX), lax.rem(peer, NX))

    def along_z(step):
        return (lax.rem(z + step, NZ) * PLANE + place, coarse)

    def rows(face):
        return pl.ds(face * FACE, FACE)

    def remote(src, dst, send, recv, device):
        return pltpu.make_async_remote_copy(
            src_ref=src, dst_ref=dst, send_sem=send, recv_sem=recv, device_id=device, device_id_type=MESH
        )

    def drain(ref, sem):
        pltpu.make_async_copy(ref, ref, sem).wait()

    def send_faces(src, dst, send, recv):
        copies = [None] * 4
        for face in range(4):
            there = partner_face[face]
            copy = remote(
                src.at[rows(face)], dst.at[rows(there)], send.at[face], recv.at[there], neighbours[face]
            )
            copy.start()
            copies[there] = copy
        return copies

    def difference(mine, theirs, face):
        value = mine - theirs
        return value if paired[face] is None else jnp.where(paired[face], value, 0.0)

    fetches = [
        pltpu.make_async_copy(source.at[0], dual, fetch_sem.at[0]),
        pltpu.make_async_copy(dirichlet.at[0], raw_dirichlet, fetch_sem.at[1]),
        pltpu.make_async_copy(neumann.at[0], raw_neumann, fetch_sem.at[2]),
    ]
    for fetch in fetches:
        fetch.start()
    barrier = pltpu.get_barrier_semaphore()

    def greet_group(step, carry):
        pl.semaphore_signal(barrier, inc=1, device_id=in_group(step)[1], device_id_type=MESH)
        return carry

    def greet_z(step, carry):
        pl.semaphore_signal(barrier, inc=1, device_id=along_z(step), device_id_type=MESH)
        return carry

    pl.semaphore_signal(barrier, inc=1, device_id=left, device_id_type=MESH)
    pl.semaphore_signal(barrier, inc=1, device_id=right, device_id_type=MESH)
    lax.fori_loop(1, GROUP, greet_group, 0)
    lax.fori_loop(1, NZ, greet_z, 0)

    lanes = lax.broadcasted_iota(jnp.int32, (1, 64), 1)
    down = lax.broadcasted_iota(jnp.int32, (256, 256), 0)
    for i in range(2):
        target = jnp.concatenate([lanes, face_map[0, i : i + 1, :] + 64], axis=1)
        perms[i] = (jnp.broadcast_to(target, (256, 256)) == down).astype(F32).astype(BF16)
    windows = (pl.ds(128, 256), pl.ds(512, 256))

    across = lax.broadcasted_iota(jnp.int32, (128, M), 0)
    scattered = jnp.zeros((128, M), F32)
    for j in range(4):
        scattered += jnp.where(across == corner_map[0, j] - BASE * z + NX, coupling[0, j : j + 1, :], 0.0)
    frame[...] = scattered.T
    for i in range(2):
        frame[windows[i], :] = permuted(perms[i], frame[windows[i], :])
    for face in range(4):
        value = frame[rows(face), :]
        if face == 0:
            value = jnp.where(place == 0, pltpu.roll(value, BASE, 1), value)
        if face == 1:
            value = jnp.where(place == PLANE - 1, pltpu.roll(value, 128 - BASE, 1), value)
        corner_out[face] = value[: FACE // 2] + pltpu.roll(value[FACE // 2 :], 64, 1)

    fetches[0].wait()
    for i in range(2):
        dual[windows[i], :] = permuted(perms[i], dual[windows[i], :])

    pl.semaphore_wait(barrier, GROUP - 1 + NZ - 1 + 2)

    faces = send_faces(dual, local_in, face_send, source_recv)
    corners = [None] * 4
    for face in range(4):
        there = partner_face[face]
        copy = remote(
            corner_out.at[face], corner_in.at[there], corner_send.at[face], corner_recv.at[there], neighbours[face]
        )
        copy.start()
        corners[there] = copy

    blocks[coarse, 0:129, :] = coarse_inverse[...]
    blocks[coarse, 129:144, :] = jnp.zeros((15, 516), F32)
    assembled[...] = jnp.zeros((WIDE, WIDE), F32)
    solved[...] = jnp.zeros((M, K), F32)
    search[...] = jnp.zeros((M, K), F32)
    image[...] = jnp.zeros((M, K), F32)
    scalars[...] = jnp.ones((8, K), F32)
    shifted[...] = jnp.zeros((7, 8, 128), F32)

    def reorder(raw, out, first):
        for i in range(2):
            raw[windows[i], :] = dot(perms[i], raw[windows[i], :]).astype(BF16)
        out[pl.ds(first, M), 0:128] = raw[:, 0:128]
        out[pl.ds(first, M), 384:512] = raw[:, 384:512]
        for i in range(2):
            out[pl.ds(first, M), windows[i]] = dot_nt(raw[:, windows[i]], perms[i]).astype(BF16)

    fetches[1].wait()
    reorder(raw_dirichlet, dirichlet_all, 128)
    fetches[2].wait()
    reorder(raw_neumann, neumann_own, 0)

    for face in range(4):
        faces[face].wait_recv()
        residual[rows(face), :] = difference(dual[rows(face), :], local_in[rows(face), :], face)

    low_lane = lax.broadcasted_iota(jnp.int32, (FACE // 2, 128), 1) < 64
    for face in range(4):
        corners[face].wait_recv()
        packed = corner_in[face]
        theirs = jnp.concatenate(
            [jnp.where(low_lane, packed, 0.0), jnp.where(low_lane, pltpu.roll(packed, 64, 1), 0.0)], axis=0
        )
        frame[rows(face), :] = difference(frame[rows(face), :], theirs, face)
    jumped = frame[...]
    high = rounded(jumped)
    low = jumped - high
    spread[...] = jnp.concatenate([high + pltpu.roll(low, 64, 1), high], axis=1).astype(BF16)
    jumped_t = jumped.T[0:64]
    high_t = rounded(jumped_t)
    product = dot(
        jnp.concatenate([high_t, jumped_t - high_t], axis=0).astype(BF16), dirichlet_all[pl.ds(128, M), :]
    )
    product = product[0:64] + product[64:128]
    high_t = rounded(product)
    dirichlet_all[0:128, :] = jnp.concatenate([high_t, product - high_t], axis=0).astype(BF16)
    for face in range(4):
        faces[face].wait_send()
        corners[face].wait_send()

    lane = lax.broadcasted_iota(jnp.int32, (8, 128), 1)

    def iteration(k, carry):
        scaled = (0.5 * residual[...]).astype(BF16)
        weighted[...] = dot(dirichlet_all[pl.ds(128, M), :], scaled)
        weighted_copies = send_faces(weighted, weighted_in, face_send, weighted_recv)
        load = dot(dirichlet_all[0:128, :], scaled)
        load = 0.5 * (load[0:64] + load[64:128])
        load = jnp.concatenate([load, jnp.zeros((64, K), F32)], axis=0)
        loads_out[...] = load.T.reshape(GROUP, 8, 128)
        loads_in[own] = loads_out[own]

        def send_load(step, carry):
            peer, device = in_group(step)
            remote(loads_out.at[peer], loads_in.at[own], group_send, loads_recv, device).start()
            return carry

        lax.fori_loop(1, GROUP, send_load, 0)

        @pl.when(k == 0)
        def _():
            half = pl.ds(pl.multiple_of(core * 72, 8), 72)
            for step in range(1, NX):
                device = (region, lax.rem(coarse + step, NX))
                remote(
                    blocks.at[coarse, half], blocks.at[coarse, half], block_send.at[step], block_recv.at[step], device
                ).start()

        u = weighted[...]
        first_sum = jnp.sum(residual[...] * u, axis=0, keepdims=True)
        second_sum = jnp.sum(image[...] * u, axis=0, keepdims=True)

        drain(loads_in.at[pl.ds(0, GROUP - 1)], loads_recv)
        plane_loads[...] = jnp.sum(loads_in[...], axis=0)
        all_loads[k, z] = plane_loads[...]

        def send_plane(i, carry):
            step = 8 + jnp.where(lax.rem(i, 2) == 1, -lax.div(i + 1, 2), lax.div(i, 2))
            remote(plane_loads, all_loads.at[k, z], plane_send, all_recv.at[k], along_z(step)).start()
            return carry

        lax.fori_loop(0, NZ - 1, send_plane, 0)

        for face in range(4):
            weighted_copies[face].wait_recv()
            dual[rows(face), :] = 0.5 * difference(weighted[rows(face), :], weighted_in[rows(face), :], face)
        local[...] = dot(neumann_own[...], dual[...].astype(BF16))
        for face in range(4):
            weighted_copies[face].wait_send()
        local_copies = send_faces(local, local_in, face_send, local_recv)
        third_sum = jnp.sum(dual[...] * local[...], axis=0, keepdims=True)
        dots_out[...] = jnp.concatenate(
            [v[:, h : h + 128] for v in (third_sum, first_sum, second_sum) for h in (0, 128)]
            + [jnp.zeros((2, 128), F32)],
            axis=0,
        )
        all_dots[k, z] = dots_out[...]

        def send_dots(i, carry):
            step = 8 + jnp.where(lax.rem(i, 2) == 1, -lax.div(i + 1, 2), lax.div(i, 2))
            remote(dots_out, all_dots.at[k, z], dots_send, dots_recv.at[k], along_z(step)).start()
            return carry

        lax.fori_loop(0, NZ - 1, send_dots, 0)

        @pl.when(k == 0)
        def _():
            half = pl.ds(pl.multiple_of(core * 72, 8), 72)
            other = (region + 1 - 2 * core, coarse)
            here = [lax.rem(coarse + NX - step, NX) for step in range(1, NX)]
            copies = [
                remote(blocks.at[i, half], blocks.at[i, half], core_send.at[s], core_recv.at[s], other)
                for s, i in enumerate(here)
            ]
            for step in range(1, NX):
                remote(
                    blocks.at[coarse, half],
                    blocks.at[here[step - 1], half],
                    block_send.at[step],
                    block_recv.at[step],
                    other,
                ).wait_recv()
                copies[step - 1].start()
            for copy in copies:
                copy.wait()
            for step in range(1, NX):
                drain(blocks.at[coarse, half], block_send.at[step])
            for i in range(NX):
                assembled[129 * i : 129 * (i + 1), 0:516] = blocks[i, 0:129, :]
            whole = assembled[...]
            inverse_high[...] = whole.astype(BF16)
            inverse_low[...] = (whole - rounded(whole)).astype(BF16)

        drain(all_loads.at[k, pl.ds(0, NZ - 1)], all_recv.at[k])
        part = [all_loads[k, i] for i in range(NZ)]
        tiles = []
        for t in range(5):
            tile = jnp.zeros((8, 128), F32)
            if t < 4:
                tile += jnp.where(lane < 124, pltpu.roll(part[4 * t], 124, 1), 0.0)
                tile += pltpu.roll(part[4 * t + 1], 28, 1) + pltpu.roll(part[4 * t + 2], 60, 1)
                tile += jnp.where(lane >= 64, pltpu.roll(part[4 * t + 3], 92, 1), 0.0)
            if t < 3:
                tile += jnp.where(lane >= 124, pltpu.roll(part[4 * t + 4], 124, 1), 0.0)
            if t > 0:
                tile += jnp.where(lane < 64, pltpu.roll(part[4 * t - 1], 92, 1), 0.0)
            tiles.append(tile)
        totals = jnp.concatenate(tiles, axis=1)
        high = rounded(totals)
        both = jnp.concatenate([high, totals - high], axis=0).astype(BF16)
        values = dot(both, inverse_high[...]) + dot(both, inverse_low[...])
        values = values[0:8] + values[8:16]
        energy = jnp.sum(totals * values, axis=1, keepdims=True)
        for t in range(5):
            shifted[t + 1] = values[:, 128 * t : 128 * (t + 1)]
        quarter, turn = lax.div(z, 4), lax.rem(z, 4)
        now, nearby, later = shifted[quarter], shifted[quarter + 1], shifted[quarter + 2]
        framed = jnp.where(
            turn == 0,
            jnp.where(lane < 4, pltpu.roll(now, 4, 1), pltpu.roll(nearby, 4, 1)),
            jnp.where(
                turn == 1,
                pltpu.roll(nearby, 100, 1),
                jnp.where(
                    turn == 2,
                    pltpu.roll(nearby, 68, 1),
                    jnp.where(lane < 36, pltpu.roll(nearby, 36, 1), pltpu.roll(later, 36, 1)),
                ),
            ),
        )
        framed = jnp.where(lane < USED, framed, jnp.where(lane == USED, energy, 0.0))

        drain(all_dots.at[k, pl.ds(0, NZ - 1)], dots_recv.at[k])
        back_out[0:8] = framed
        back_out[8:16] = jnp.sum(all_dots[k], axis=0)
        back_in[own] = back_out[...]

        def send_back(step, carry):
            device = in_group(step)[1]
            remote(back_out, back_in.at[own], back_send, back_recv, device).start()
            return carry

        lax.fori_loop(1, GROUP, send_back, 0)

        for face in range(4):
            local_copies[face].wait_recv()
        drain(back_in.at[pl.ds(0, GROUP - 1)], back_recv)
        coarse_values = back_in[:, 0:8, :].reshape(K, 128).T
        sums = jnp.sum(back_in[:, 8:16, :], axis=0)

        def joined(i):
            return jnp.concatenate([sums[i : i + 1], sums[i + 1 : i + 2]], axis=1)

        curve = 2.0 * (joined(0) + coarse_values[USED : USED + 1])
        product_sum = joined(2)
        ratio = jnp.where(k > 0, product_sum / scalars[0:1], 0.0)
        curve = curve + 2.0 * ratio * joined(4)
        curve = curve + jnp.where(k > 0, ratio * ratio * scalars[1:2], 0.0)
        step_len = product_sum / curve
        scalars[0:1] = product_sum
        scalars[1:2] = curve
        values_high = rounded(coarse_values[0:64])
        stacked = jnp.concatenate(
            [values_high, values_high, coarse_values[0:64] - values_high, jnp.zeros((64, K), F32)], axis=0
        ).astype(BF16)
        for face in range(4):
            at = rows(face)
            own_image = difference(local[at, :], local_in[at, :], face) + dot(spread[at, :], stacked)
            new_image = own_image + ratio * image[at, :]
            new_search = dual[at, :] + ratio * search[at, :]
            image[at, :] = new_image
            search[at, :] = new_search
            solved[at, :] += step_len * new_search
            residual[at, :] -= step_len * new_image

        for face in range(4):
            local_copies[face].wait_send()
        drain(loads_out.at[pl.ds(0, GROUP - 1)], group_send)
        drain(all_loads.at[k, pl.ds(0, NZ - 1)], plane_send)
        drain(all_dots.at[k, pl.ds(0, NZ - 1)], dots_send)
        drain(back_in.at[pl.ds(0, GROUP - 1)], back_send)
        return carry

    lax.fori_loop(0, ITERS, iteration, 0)

    for value, out in ((solved, x_out), (residual, r_out)):
        out[0, 0:128, :] = value[0:128, :]
        out[0, 384:512, :] = value[384:512, :]
        for i in range(2):
            out[0, windows[i], :] = permuted(perms[i].astype(F32).T.astype(BF16), value[windows[i], :])


def body(source, neumann, dirichlet, coupling, corner_map, face_map, coarse_inverse):
    field = pltpu.VMEM((M, K), F32)
    square = pltpu.VMEM((M, M), BF16)
    dma, one = pltpu.SemaphoreType.DMA, pltpu.SemaphoreType.DMA(())
    scratch = [
        field, field, field, field, field, field, field,
        field, field,
        pltpu.VMEM((4, FACE // 2, 128), F32), pltpu.VMEM((4, FACE // 2, 128), F32), pltpu.VMEM((M, 128), F32),
        pltpu.VMEM((2, 256, 256), BF16), pltpu.VMEM((M + 128, M), BF16), square, square, square,
        pltpu.VMEM((M, 256), BF16),
        pltpu.VMEM((NX, 144, 516), F32), pltpu.VMEM((WIDE, WIDE), F32),
        pltpu.VMEM((WIDE, WIDE), BF16), pltpu.VMEM((WIDE, WIDE), BF16),
        pltpu.VMEM((7, 8, 128), F32), pltpu.VMEM((8, K), F32),
        pltpu.VMEM((GROUP, 8, 128), F32), pltpu.VMEM((GROUP, 8, 128), F32),
        pltpu.VMEM((8, 128), F32), pltpu.VMEM((ITERS, NZ, 8, 128), F32),
        pltpu.VMEM((8, 128), F32), pltpu.VMEM((ITERS, NZ, 8, 128), F32),
        pltpu.VMEM((16, 128), F32), pltpu.VMEM((GROUP, 16, 128), F32),
        dma((3,)), dma((4,)), dma((4,)), dma((4,)), dma((4,)), dma((4,)), dma((4,)),
        dma((4,)), dma((4,)), dma((3,)), dma((3,)),
        one, one, one, dma((ITERS,)), one, dma((ITERS,)), one, one,
    ]
    vmem, hbm = pl.BlockSpec(memory_space=pltpu.VMEM), pl.BlockSpec(memory_space=pl.ANY)
    return pl.pallas_call(
        kernel,
        out_shape=(jax.ShapeDtypeStruct((1, M, K), F32), jax.ShapeDtypeStruct((1, M, K), F32)),
        in_specs=[hbm, hbm, hbm, vmem, pl.BlockSpec(memory_space=pltpu.SMEM), vmem, vmem],
        out_specs=(vmem, vmem),
        scratch_shapes=scratch,
        compiler_params=pltpu.CompilerParams(collective_id=0, has_side_effects=True, vmem_limit_bytes=48 * 2**20),
        cost_estimate=pl.CostEstimate(flops=3 * 4 * M * M * K, bytes_accessed=6 * 10**6, transcendentals=0),
    )(source, neumann, dirichlet, coupling, corner_map, face_map, coarse_inverse)


def solution(mesh):
    split = P(("region", "coarse"), None, None)
    placed = (split, split, split, split, P(("region", "coarse"), None), split, P("coarse", None))
    return jax.shard_map(body, mesh=mesh, in_specs=placed, out_specs=(split, split), check_vma=False)
```

```python
import functools

import jax
import jax.numpy as jnp
from jax import lax
from jax.experimental import pallas as pl
from jax.experimental.pallas import tpu as pltpu
from jax.sharding import PartitionSpec as P

ITERS = 3
MESH = pl.DeviceIdType.MESH
F32, BF16 = jnp.float32, jnp.bfloat16

PLANE = 8
NX = 4
GROUP = PLANE * NX
NZ = 16
FACE = 192
M = 4 * FACE
K = 256
BASE = NX * PLANE
USED = NX * (PLANE + 3)
WIDE = 640


def hops(step):
    return min(step, 4 - step)


MEMBERS = sorted(
    ((dy, dx, dc) for dy in range(4) for dx in range(4) for dc in range(2) if (dy, dx, dc) != (0, 0, 0)),
    key=lambda d: (-hops(d[0]) - hops(d[1]), d),
)
PLANES = sorted(range(1, NZ), key=lambda step: -min(step, NZ - step))


def rounded(value):
    return value.astype(BF16).astype(F32)


def dot(a, b):
    return jnp.dot(a, b, preferred_element_type=F32)


def dot_nt(a, b):
    return lax.dot_general(a, b, (((1,), (1,)), ((), ())), preferred_element_type=F32)


def permuted(onehot, value):
    high = value.astype(BF16)
    rest = value - high.astype(F32)
    middle = rest.astype(BF16)
    low = (rest - middle.astype(F32)).astype(BF16)
    return (dot(onehot, high) + dot(onehot, middle)) + dot(onehot, low)


def kernel(
    source, neumann, dirichlet, coupling, corner_map, face_map, coarse_inverse,
    x_out, r_out,
    residual, solved, search, image, weighted, dual, local,
    weighted_in, local_in, corner_out, corner_in, frame,
    perms, dirichlet_all, neumann_own, raw_dirichlet, raw_neumann, spread,
    blocks, assembled, inverse_high, inverse_low, shifted, scalars,
    loads_out, loads_in, plane_loads, all_loads, dots_out, all_dots, back_out, back_in,
    fetch_sem, face_send, source_recv, weighted_recv, local_recv, corner_send, corner_recv,
    block_send, block_recv, core_send, core_recv,
    group_send, loads_recv, plane_send, all_recv, dots_send, dots_recv, back_send, back_recv,
):
    region, coarse = lax.axis_index("region"), lax.axis_index("coarse")
    z, place = lax.div(region, PLANE), lax.rem(region, PLANE)
    core = lax.rem(region, 2)
    own = place * NX + coarse
    n_region = NZ * PLANE
    left = (lax.rem(region + n_region - 1, n_region), coarse)
    right = (lax.rem(region + 1, n_region), coarse)
    before = (region, lax.rem(coarse + NX - 1, NX))
    after = (region, lax.rem(coarse + 1, NX))
    neighbours = (left, right, before, after)
    partner_face = (1, 0, 3, 2)
    paired = (region > 0, region < n_region - 1, None, None)

    row = lax.div(place, 2)
    members = []
    for dy, dx, dc in MEMBERS:
        there = 2 * lax.rem(row + dy, 4) + (1 - core if dc else core)
        x = lax.rem(coarse + dx, NX)
        members.append((there * NX + x, (z * PLANE + there, x)))
    planes = [(lax.rem(z + step, NZ) * PLANE + place, coarse) for step in PLANES]

    def rows(face):
        return pl.ds(face * FACE, FACE)

    def remote(src, dst, send, recv, device):
        return pltpu.make_async_remote_copy(
            src_ref=src, dst_ref=dst, send_sem=send, recv_sem=recv, device_id=device, device_id_type=MESH
        )

    def drain(ref, sem):
        pltpu.make_async_copy(ref, ref, sem).wait()

    def send_faces(src, dst, send, recv):
        copies = [None] * 4
        for face in range(4):
            there = partner_face[face]
            copy = remote(
                src.at[rows(face)], dst.at[rows(there)], send.at[face], recv.at[there], neighbours[face]
            )
            copy.start()
            copies[there] = copy
        return copies

    def difference(mine, theirs, face):
        value = mine - theirs
        return value if paired[face] is None else jnp.where(paired[face], value, 0.0)

    fetches = [
        pltpu.make_async_copy(source.at[0], dual, fetch_sem.at[0]),
        pltpu.make_async_copy(dirichlet.at[0], raw_dirichlet, fetch_sem.at[1]),
        pltpu.make_async_copy(neumann.at[0], raw_neumann, fetch_sem.at[2]),
    ]
    for fetch in fetches:
        fetch.start()
    barrier = pltpu.get_barrier_semaphore()

    for device in planes + [device for _, device in members] + [left, right]:
        pl.semaphore_signal(barrier, inc=1, device_id=device, device_id_type=MESH)

    lanes = lax.broadcasted_iota(jnp.int32, (1, 64), 1)
    down = lax.broadcasted_iota(jnp.int32, (256, 256), 0)
    for i in range(2):
        target = jnp.concatenate([lanes, face_map[0, i : i + 1, :] + 64], axis=1)
        perms[i] = (jnp.broadcast_to(target, (256, 256)) == down).astype(F32).astype(BF16)
    windows = (pl.ds(128, 256), pl.ds(512, 256))

    across = lax.broadcasted_iota(jnp.int32, (128, M), 0)
    scattered = jnp.zeros((128, M), F32)
    for j in range(4):
        scattered += jnp.where(across == corner_map[0, j] - BASE * z + NX, coupling[0, j : j + 1, :], 0.0)
    frame[...] = scattered.T
    for i in range(2):
        frame[windows[i], :] = permuted(perms[i], frame[windows[i], :])
    for face in range(4):
        value = frame[rows(face), :]
        if face == 0:
            value = jnp.where(place == 0, pltpu.roll(value, BASE, 1), value)
        if face == 1:
            value = jnp.where(place == PLANE - 1, pltpu.roll(value, 128 - BASE, 1), value)
        corner_out[face] = value[: FACE // 2] + pltpu.roll(value[FACE // 2 :], 64, 1)

    fetches[0].wait()
    for i in range(2):
        dual[windows[i], :] = permuted(perms[i], dual[windows[i], :])

    pl.semaphore_wait(barrier, GROUP - 1 + NZ - 1 + 2)

    corners = [None] * 4
    for face in range(4):
        there = partner_face[face]
        copy = remote(
            corner_out.at[face], corner_in.at[there], corner_send.at[face], corner_recv.at[there], neighbours[face]
        )
        copy.start()
        corners[there] = copy
    faces = send_faces(dual, local_in, face_send, source_recv)
    half = pl.ds(pl.multiple_of(core * 72, 8), 72)

    def block_copy(i, sem, device):
        return remote(blocks.at[i, half], blocks.at[i, half], block_send.at[sem], block_recv.at[sem], device)

    blocks[coarse, 0:129, :] = coarse_inverse[...]
    blocks[coarse, 129:144, :] = jnp.zeros((15, 516), F32)
    block_copy(coarse, 0, after).start()
    block_copy(coarse, 1, before).start()
    assembled[...] = jnp.zeros((WIDE, WIDE), F32)
    solved[...] = jnp.zeros((M, K), F32)
    search[...] = jnp.zeros((M, K), F32)
    image[...] = jnp.zeros((M, K), F32)
    scalars[...] = jnp.ones((8, K), F32)
    shifted[...] = jnp.zeros((7, 8, 128), F32)

    def reorder(raw, out, first):
        for i in range(2):
            raw[windows[i], :] = dot(perms[i], raw[windows[i], :]).astype(BF16)
        out[pl.ds(first, M), 0:128] = raw[:, 0:128]
        out[pl.ds(first, M), 384:512] = raw[:, 384:512]
        for i in range(2):
            out[pl.ds(first, M), windows[i]] = dot_nt(raw[:, windows[i]], perms[i]).astype(BF16)

    fetches[1].wait()
    reorder(raw_dirichlet, dirichlet_all, 128)
    fetches[2].wait()
    reorder(raw_neumann, neumann_own, 0)

    low_lane = lax.broadcasted_iota(jnp.int32, (FACE // 2, 128), 1) < 64
    for face in range(4):
        corners[face].wait_recv()
        packed = corner_in[face]
        theirs = jnp.concatenate(
            [jnp.where(low_lane, packed, 0.0), jnp.where(low_lane, pltpu.roll(packed, 64, 1), 0.0)], axis=0
        )
        frame[rows(face), :] = difference(frame[rows(face), :], theirs, face)
    jumped = frame[...]
    high = rounded(jumped)
    low = jumped - high
    spread[...] = jnp.concatenate([high + pltpu.roll(low, 64, 1), high], axis=1).astype(BF16)
    jumped_t = jumped.T[0:64]
    high_t = rounded(jumped_t)
    product = dot(
        jnp.concatenate([high_t, jumped_t - high_t], axis=0).astype(BF16), dirichlet_all[pl.ds(128, M), :]
    )
    product = product[0:64] + product[64:128]
    high_t = rounded(product)
    dirichlet_all[0:128, :] = jnp.concatenate([high_t, product - high_t], axis=0).astype(BF16)
    for face in range(4):
        faces[face].wait_recv()
        residual[rows(face), :] = difference(dual[rows(face), :], local_in[rows(face), :], face)
    for face in range(4):
        faces[face].wait_send()
        corners[face].wait_send()

    lane = lax.broadcasted_iota(jnp.int32, (8, 128), 1)

    def update():
        for face in range(4):
            at = rows(face)
            new_search = dual[at, :] + scalars[2:3] * search[at, :]
            search[at, :] = new_search
            solved[at, :] += scalars[3:4] * new_search

    def iteration(k, carry):
        scaled = (0.5 * residual[...]).astype(BF16)
        load = dot(dirichlet_all[0:128, :], scaled)
        load = 0.5 * (load[0:64] + load[64:128])
        load = jnp.concatenate([load, jnp.zeros((64, K), F32)], axis=0)
        loads_out[...] = load.T.reshape(GROUP, 8, 128)
        loads_in[own] = loads_out[own]

        for peer, device in members:
            remote(loads_out.at[peer], loads_in.at[own], group_send, loads_recv, device).start()
        weighted[...] = dot(dirichlet_all[pl.ds(128, M), :], scaled)
        weighted_copies = send_faces(weighted, weighted_in, face_send, weighted_recv)

        @pl.when(k > 0)
        def _():
            update()

        @pl.when(k == 0)
        def _():
            for sem in range(2):
                block_copy(coarse, sem, after).wait()
            turn = 1 - 2 * core
            block_copy(lax.rem(coarse + NX - turn, NX), 2, (region, lax.rem(coarse + NX + turn, NX))).start()

        u = weighted[...]
        first_sum = jnp.sum(residual[...] * u, axis=0, keepdims=True)
        second_sum = jnp.sum(image[...] * u, axis=0, keepdims=True)

        drain(loads_in.at[pl.ds(0, GROUP - 1)], loads_recv)
        plane_loads[...] = jnp.sum(loads_in[...], axis=0)
        all_loads[k, z] = plane_loads[...]

        for device in planes:
            remote(plane_loads, all_loads.at[k, z], plane_send, all_recv.at[k], device).start()

        for face in range(4):
            weighted_copies[face].wait_recv()
            dual[rows(face), :] = 0.5 * difference(weighted[rows(face), :], weighted_in[rows(face), :], face)
        local[...] = dot(neumann_own[...], dual[...].astype(BF16))
        for face in range(4):
            weighted_copies[face].wait_send()
        third_sum = jnp.sum(dual[...] * local[...], axis=0, keepdims=True)
        dots_out[...] = jnp.concatenate(
            [v[:, h : h + 128] for v in (third_sum, first_sum, second_sum) for h in (0, 128)]
            + [jnp.zeros((2, 128), F32)],
            axis=0,
        )
        all_dots[k, z] = dots_out[...]

        for device in planes:
            remote(dots_out, all_dots.at[k, z], dots_send, dots_recv.at[k], device).start()
        local_copies = send_faces(local, local_in, face_send, local_recv)

        @pl.when(k == 0)
        def _():
            block_copy(coarse, 2, after).wait()
            other = (region + 1 - 2 * core, coarse)
            copies = []
            for step in range(1, NX):
                i = lax.rem(coarse + step, NX)
                copies.append(
                    remote(
                        blocks.at[i, half], blocks.at[i, half], core_send.at[step - 1], core_recv.at[step - 1], other
                    )
                )
                copies[-1].start()
            for copy in copies:
                copy.wait()
            for i in range(NX):
                assembled[129 * i : 129 * (i + 1), 0:516] = blocks[i, 0:129, :]
            whole = assembled[...]
            inverse_high[...] = whole.astype(BF16)
            inverse_low[...] = (whole - rounded(whole)).astype(BF16)

        drain(all_loads.at[k, pl.ds(0, NZ - 1)], all_recv.at[k])
        part = [all_loads[k, i] for i in range(NZ)]
        tiles = []
        for t in range(5):
            tile = jnp.zeros((8, 128), F32)
            if t < 4:
                tile += jnp.where(lane < 124, pltpu.roll(part[4 * t], 124, 1), 0.0)
                tile += pltpu.roll(part[4 * t + 1], 28, 1) + pltpu.roll(part[4 * t + 2], 60, 1)
                tile += jnp.where(lane >= 64, pltpu.roll(part[4 * t + 3], 92, 1), 0.0)
            if t < 3:
                tile += jnp.where(lane >= 124, pltpu.roll(part[4 * t + 4], 124, 1), 0.0)
            if t > 0:
                tile += jnp.where(lane < 64, pltpu.roll(part[4 * t - 1], 92, 1), 0.0)
            tiles.append(tile)
        totals = jnp.concatenate(tiles, axis=1)
        high = rounded(totals)
        both = jnp.concatenate([high, totals - high], axis=0).astype(BF16)
        values = dot(both, inverse_high[...]) + dot(both, inverse_low[...])
        values = values[0:8] + values[8:16]
        energy = jnp.sum(totals * values, axis=1, keepdims=True)
        for t in range(5):
            shifted[t + 1] = values[:, 128 * t : 128 * (t + 1)]
        quarter, turn = lax.div(z, 4), lax.rem(z, 4)
        now, nearby, later = shifted[quarter], shifted[quarter + 1], shifted[quarter + 2]
        framed = jnp.where(
            turn == 0,
            jnp.where(lane < 4, pltpu.roll(now, 4, 1), pltpu.roll(nearby, 4, 1)),
            jnp.where(
                turn == 1,
                pltpu.roll(nearby, 100, 1),
                jnp.where(
                    turn == 2,
                    pltpu.roll(nearby, 68, 1),
                    jnp.where(lane < 36, pltpu.roll(nearby, 36, 1), pltpu.roll(later, 36, 1)),
                ),
            ),
        )
        framed = jnp.where(lane < USED, framed, jnp.where(lane == USED, energy, 0.0))

        drain(all_dots.at[k, pl.ds(0, NZ - 1)], dots_recv.at[k])
        back_out[0:8] = framed
        back_out[8:16] = jnp.sum(all_dots[k], axis=0)
        back_in[own] = back_out[...]

        for _, device in members:
            remote(back_out, back_in.at[own], back_send, back_recv, device).start()

        for face in range(4):
            local_copies[face].wait_send()
        for face in range(4):
            local_copies[face].wait_recv()
            local[rows(face), :] = difference(local[rows(face), :], local_in[rows(face), :], face)
        drain(back_in.at[pl.ds(0, GROUP - 1)], back_recv)
        coarse_values = back_in[:, 0:8, :].reshape(K, 128).T
        sums = jnp.sum(back_in[:, 8:16, :], axis=0)

        def joined(i):
            return jnp.concatenate([sums[i : i + 1], sums[i + 1 : i + 2]], axis=1)

        curve = 2.0 * (joined(0) + coarse_values[USED : USED + 1])
        product_sum = joined(2)
        ratio = jnp.where(k > 0, product_sum / scalars[0:1], 0.0)
        curve = curve + 2.0 * ratio * joined(4)
        curve = curve + jnp.where(k > 0, ratio * ratio * scalars[1:2], 0.0)
        step_len = product_sum / curve
        scalars[0:1] = product_sum
        scalars[1:2] = curve
        values_high = rounded(coarse_values[0:64])
        stacked = jnp.concatenate(
            [values_high, values_high, coarse_values[0:64] - values_high, jnp.zeros((64, K), F32)], axis=0
        ).astype(BF16)
        scalars[2:3] = ratio
        scalars[3:4] = step_len
        for face in range(4):
            at = rows(face)
            new_image = local[at, :] + dot(spread[at, :], stacked) + ratio * image[at, :]
            image[at, :] = new_image
            residual[at, :] -= step_len * new_image

        drain(loads_out.at[pl.ds(0, GROUP - 1)], group_send)
        drain(all_loads.at[k, pl.ds(0, NZ - 1)], plane_send)
        drain(all_dots.at[k, pl.ds(0, NZ - 1)], dots_send)
        drain(back_in.at[pl.ds(0, GROUP - 1)], back_send)
        return carry

    lax.fori_loop(0, ITERS, iteration, 0)
    update()

    for value, out in ((solved, x_out), (residual, r_out)):
        out[0, 0:128, :] = value[0:128, :]
        out[0, 384:512, :] = value[384:512, :]
        for i in range(2):
            out[0, windows[i], :] = permuted(perms[i].astype(F32).T.astype(BF16), value[windows[i], :])


def body(source, neumann, dirichlet, coupling, corner_map, face_map, coarse_inverse):
    field = pltpu.VMEM((M, K), F32)
    square = pltpu.VMEM((M, M), BF16)
    dma, one = pltpu.SemaphoreType.DMA, pltpu.SemaphoreType.DMA(())
    scratch = [
        field, field, field, field, field, field, field,
        field, field,
        pltpu.VMEM((4, FACE // 2, 128), F32), pltpu.VMEM((4, FACE // 2, 128), F32), pltpu.VMEM((M, 128), F32),
        pltpu.VMEM((2, 256, 256), BF16), pltpu.VMEM((M + 128, M), BF16), square, square, square,
        pltpu.VMEM((M, 256), BF16),
        pltpu.VMEM((NX, 144, 516), F32), pltpu.VMEM((WIDE, WIDE), F32),
        pltpu.VMEM((WIDE, WIDE), BF16), pltpu.VMEM((WIDE, WIDE), BF16),
        pltpu.VMEM((7, 8, 128), F32), pltpu.VMEM((8, K), F32),
        pltpu.VMEM((GROUP, 8, 128), F32), pltpu.VMEM((GROUP, 8, 128), F32),
        pltpu.VMEM((8, 128), F32), pltpu.VMEM((ITERS, NZ, 8, 128), F32),
        pltpu.VMEM((8, 128), F32), pltpu.VMEM((ITERS, NZ, 8, 128), F32),
        pltpu.VMEM((16, 128), F32), pltpu.VMEM((GROUP, 16, 128), F32),
        dma((3,)), dma((4,)), dma((4,)), dma((4,)), dma((4,)), dma((4,)), dma((4,)),
        dma((3,)), dma((3,)), dma((3,)), dma((3,)),
        one, one, one, dma((ITERS,)), one, dma((ITERS,)), one, one,
    ]
    vmem, hbm = pl.BlockSpec(memory_space=pltpu.VMEM), pl.BlockSpec(memory_space=pl.ANY)
    return pl.pallas_call(
        kernel,
        out_shape=(jax.ShapeDtypeStruct((1, M, K), F32), jax.ShapeDtypeStruct((1, M, K), F32)),
        in_specs=[hbm, hbm, hbm, vmem, pl.BlockSpec(memory_space=pltpu.SMEM), vmem, vmem],
        out_specs=(vmem, vmem),
        scratch_shapes=scratch,
        compiler_params=pltpu.CompilerParams(collective_id=0, has_side_effects=True, vmem_limit_bytes=62 * 2**20),
        cost_estimate=pl.CostEstimate(flops=3 * 4 * M * M * K, bytes_accessed=6 * 10**6, transcendentals=0),
    )(source, neumann, dirichlet, coupling, corner_map, face_map, coarse_inverse)


def solution(mesh):
    split = P(("region", "coarse"), None, None)
    placed = (split, split, split, split, P(("region", "coarse"), None), split, P("coarse", None))
    return jax.shard_map(body, mesh=mesh, in_specs=placed, out_specs=(split, split), check_vma=False)
```

```python
import functools

import jax
import jax.numpy as jnp
from jax import lax
from jax.experimental import pallas as pl
from jax.experimental.pallas import tpu as pltpu
from jax.sharding import PartitionSpec as P

ITERS = 3
MESH = pl.DeviceIdType.MESH
F32, BF16 = jnp.float32, jnp.bfloat16

PLANE = 8
NX = 4
GROUP = PLANE * NX
NZ = 16
FACE = 192
M = 4 * FACE
K = 256
BASE = NX * PLANE
USED = NX * (PLANE + 3)
WIDE = 640


def hops(step):
    return min(step, 4 - step)


MEMBERS = sorted(
    ((dy, dx, dc) for dy in range(4) for dx in range(4) for dc in range(2) if (dy, dx, dc) != (0, 0, 0)),
    key=lambda d: (-hops(d[0]) - hops(d[1]), d),
)
PLANES = sorted(range(1, NZ), key=lambda step: -min(step, NZ - step))


def rounded(value):
    return value.astype(BF16).astype(F32)


def dot(a, b):
    return jnp.dot(a, b, preferred_element_type=F32)


def dot_nt(a, b):
    return lax.dot_general(a, b, (((1,), (1,)), ((), ())), preferred_element_type=F32)


def permuted(onehot, value):
    high = value.astype(BF16)
    rest = value - high.astype(F32)
    middle = rest.astype(BF16)
    low = (rest - middle.astype(F32)).astype(BF16)
    return (dot(onehot, high) + dot(onehot, middle)) + dot(onehot, low)


WINDOWS = (pl.ds(128, 256), pl.ds(512, 256))


def one_hots(face_map, out):
    lanes = lax.broadcasted_iota(jnp.int32, (1, 64), 1)
    down = lax.broadcasted_iota(jnp.int32, (256, 256), 0)
    for i in range(2):
        target = jnp.concatenate([lanes, face_map[0, i : i + 1, :] + 64], axis=1)
        out[i] = (jnp.broadcast_to(target, (256, 256)) == down).astype(F32).astype(BF16)


def kernel(
    source, neumann, dirichlet, coupling_in, corner_map_in, face_map_in, coarse_inverse_in,
    solved, residual,
    coupling, corner_map, face_map, coarse_inverse, search, image, weighted, dual, local,
    weighted_in, local_in, corner_out, corner_in, frame,
    perms, dirichlet_all, neumann_own, raw_dirichlet, raw_neumann, spread,
    blocks, assembled, inverse_high, inverse_low, shifted, scalars,
    loads_out, loads_in, plane_loads, all_loads, dots_out, all_dots, back_out, back_in,
    line_sem, near_sem, far_sem, fetch_sem, face_send, source_recv, weighted_recv, local_recv, corner_send, corner_recv,
    block_send, block_recv, core_send, core_recv,
    group_send, loads_recv, plane_send, all_recv, dots_send, dots_recv, back_send, back_recv,
):
    region, coarse = lax.axis_index("region"), lax.axis_index("coarse")
    z, place = lax.div(region, PLANE), lax.rem(region, PLANE)
    core = lax.rem(region, 2)
    own = place * NX + coarse
    n_region = NZ * PLANE
    left = (lax.rem(region + n_region - 1, n_region), coarse)
    right = (lax.rem(region + 1, n_region), coarse)
    before = (region, lax.rem(coarse + NX - 1, NX))
    after = (region, lax.rem(coarse + 1, NX))
    neighbours = (left, right, before, after)
    partner_face = (1, 0, 3, 2)
    paired = (region > 0, region < n_region - 1, None, None)

    row = lax.div(place, 2)
    members = []
    for dy, dx, dc in MEMBERS:
        there = 2 * lax.rem(row + dy, 4) + (1 - core if dc else core)
        x = lax.rem(coarse + dx, NX)
        members.append((there * NX + x, (z * PLANE + there, x)))
    planes = [(lax.rem(z + step, NZ) * PLANE + place, coarse) for step in PLANES]

    def rows(face):
        return pl.ds(face * FACE, FACE)

    def remote(src, dst, send, recv, device):
        return pltpu.make_async_remote_copy(
            src_ref=src, dst_ref=dst, send_sem=send, recv_sem=recv, device_id=device, device_id_type=MESH
        )

    def drain(ref, sem):
        pltpu.make_async_copy(ref, ref, sem).wait()

    def send_faces(src, dst, send, recv):
        copies = [None] * 4
        for face in (2, 3, 0, 1):
            there = partner_face[face]
            copy = remote(
                src.at[rows(face)], dst.at[rows(there)], send.at[face], recv.at[there], neighbours[face]
            )
            copy.start()
            copies[there] = copy
        return copies

    def difference(mine, theirs, face):
        value = mine - theirs
        return value if paired[face] is None else jnp.where(paired[face], value, 0.0)

    line = [(region, lax.rem(coarse + dx, NX)) for dx in range(1, NX)]
    mates = [(z * PLANE + lax.rem(place + step, PLANE), coarse) for step in range(1, PLANE)]

    def plane_at(step):
        return (lax.rem(z + step + NZ, NZ) * PLANE + place, coarse)

    def greet(sem, devices):
        for device in devices:
            pl.semaphore_signal(sem, inc=1, device_id=device, device_id_type=MESH)

    barrier = pltpu.get_barrier_semaphore()
    first_round = [plane_at(2), plane_at(-2), plane_at(1), plane_at(-1), left, right] + line + mates
    greet(barrier, first_round)
    fetches = [
        pltpu.make_async_copy(src, dst, fetch_sem.at[i])
        for i, (src, dst) in enumerate(
            (
                (face_map_in, face_map),
                (corner_map_in, corner_map),
                (coupling_in, coupling),
                (source.at[0], dual),
                (dirichlet.at[0], raw_dirichlet),
                (neumann.at[0], raw_neumann),
                (coarse_inverse_in, coarse_inverse),
            )
        )
    ]
    for fetch in fetches:
        fetch.start()
    for fetch in fetches[0:3]:
        fetch.wait()

    one_hots(face_map, perms)

    across = lax.broadcasted_iota(jnp.int32, (128, M), 0)
    scattered = jnp.zeros((128, M), F32)
    for j in range(4):
        scattered += jnp.where(across == corner_map[0:1, j : j + 1] - BASE * z + NX, coupling[0, j : j + 1, :], 0.0)
    frame[...] = scattered.T
    for i in range(2):
        frame[WINDOWS[i], :] = permuted(perms[i], frame[WINDOWS[i], :])
    for face in range(4):
        value = frame[rows(face), :]
        if face == 0:
            value = jnp.where(place == 0, pltpu.roll(value, BASE, 1), value)
        if face == 1:
            value = jnp.where(place == PLANE - 1, pltpu.roll(value, 128 - BASE, 1), value)
        corner_out[face] = value[: FACE // 2] + pltpu.roll(value[FACE // 2 :], 64, 1)

    fetches[3].wait()
    for i in range(2):
        dual[WINDOWS[i], :] = permuted(perms[i], dual[WINDOWS[i], :])

    pl.semaphore_wait(barrier, len(first_round))

    corners = [None] * 4
    for face in range(4):
        there = partner_face[face]
        copy = remote(
            corner_out.at[face], corner_in.at[there], corner_send.at[face], corner_recv.at[there], neighbours[face]
        )
        copy.start()
        corners[there] = copy
    faces = send_faces(dual, local_in, face_send, source_recv)
    greet(line_sem, line)
    greet(near_sem, [plane_at(2), plane_at(-2)])
    half = pl.ds(pl.multiple_of(core * 72, 8), 72)

    def block_copy(i, sem, device):
        return remote(blocks.at[i, half], blocks.at[i, half], block_send.at[sem], block_recv.at[sem], device)

    fetches[6].wait()
    blocks[coarse, 0:129, :] = coarse_inverse[...]
    blocks[coarse, 129:144, :] = jnp.zeros((15, 516), F32)
    block_copy(coarse, 0, after).start()
    block_copy(coarse, 1, before).start()
    assembled[...] = jnp.zeros((WIDE, WIDE), F32)
    solved[...] = jnp.zeros((M, K), F32)
    search[...] = jnp.zeros((M, K), F32)
    image[...] = jnp.zeros((M, K), F32)
    scalars[...] = jnp.ones((8, K), F32)
    shifted[...] = jnp.zeros((7, 8, 128), F32)

    def reorder(raw, out, first):
        for i in range(2):
            raw[WINDOWS[i], :] = dot(perms[i], raw[WINDOWS[i], :]).astype(BF16)
        out[pl.ds(first, M), 0:128] = raw[:, 0:128]
        out[pl.ds(first, M), 384:512] = raw[:, 384:512]
        for i in range(2):
            out[pl.ds(first, M), WINDOWS[i]] = dot_nt(raw[:, WINDOWS[i]], perms[i]).astype(BF16)

    fetches[4].wait()
    reorder(raw_dirichlet, dirichlet_all, 128)
    fetches[5].wait()
    reorder(raw_neumann, neumann_own, 0)
    pl.semaphore_wait(near_sem, 2)
    greet(far_sem, [plane_at(4), plane_at(-4)])

    low_lane = lax.broadcasted_iota(jnp.int32, (FACE // 2, 128), 1) < 64
    for face in range(4):
        corners[face].wait_recv()
        packed = corner_in[face]
        theirs = jnp.concatenate(
            [jnp.where(low_lane, packed, 0.0), jnp.where(low_lane, pltpu.roll(packed, 64, 1), 0.0)], axis=0
        )
        frame[rows(face), :] = difference(frame[rows(face), :], theirs, face)
    jumped = frame[...]
    high = rounded(jumped)
    low = jumped - high
    spread[...] = jnp.concatenate([high + pltpu.roll(low, 64, 1), high], axis=1).astype(BF16)
    jumped_t = jumped.T[0:64]
    high_t = rounded(jumped_t)
    product = dot(
        jnp.concatenate([high_t, jumped_t - high_t], axis=0).astype(BF16), dirichlet_all[pl.ds(128, M), :]
    )
    product = product[0:64] + product[64:128]
    high_t = rounded(product)
    dirichlet_all[0:128, :] = jnp.concatenate([high_t, product - high_t], axis=0).astype(BF16)
    for face in range(4):
        faces[face].wait_recv()
        residual[rows(face), :] = difference(dual[rows(face), :], local_in[rows(face), :], face)
    for face in range(4):
        faces[face].wait_send()
        corners[face].wait_send()

    pl.semaphore_wait(line_sem, NX - 1)
    lane = lax.broadcasted_iota(jnp.int32, (8, 128), 1)

    def update():
        for face in range(4):
            at = rows(face)
            new_search = dual[at, :] + scalars[2:3] * search[at, :]
            search[at, :] = new_search
            solved[at, :] += scalars[3:4] * new_search

    def iteration(k, carry):
        scaled = (0.5 * residual[...]).astype(BF16)
        load = dot(dirichlet_all[0:128, :], scaled)
        load = 0.5 * (load[0:64] + load[64:128])
        load = jnp.concatenate([load, jnp.zeros((64, K), F32)], axis=0)
        loads_out[...] = load.T.reshape(GROUP, 8, 128)
        loads_in[own] = loads_out[own]

        for peer, device in members:
            remote(loads_out.at[peer], loads_in.at[own], group_send, loads_recv, device).start()
        weighted[...] = dot(dirichlet_all[pl.ds(128, M), :], scaled)
        weighted_copies = send_faces(weighted, weighted_in, face_send, weighted_recv)

        @pl.when(k > 0)
        def _():
            update()

        @pl.when(k == 0)
        def _():
            for sem in range(2):
                block_copy(coarse, sem, after).wait()
            turn = 1 - 2 * core
            block_copy(lax.rem(coarse + NX - turn, NX), 2, (region, lax.rem(coarse + NX + turn, NX))).start()

        u = weighted[...]
        first_sum = jnp.sum(residual[...] * u, axis=0, keepdims=True)
        second_sum = jnp.sum(image[...] * u, axis=0, keepdims=True)

        @pl.when(k == 0)
        def _():
            pl.semaphore_wait(far_sem, 2)

        drain(loads_in.at[pl.ds(0, GROUP - 1)], loads_recv)
        plane_loads[...] = jnp.sum(loads_in[...], axis=0)
        all_loads[k, z] = plane_loads[...]

        for device in planes:
            remote(plane_loads, all_loads.at[k, z], plane_send, all_recv.at[k], device).start()

        for face in range(4):
            weighted_copies[face].wait_recv()
            dual[rows(face), :] = 0.5 * difference(weighted[rows(face), :], weighted_in[rows(face), :], face)
            if face == 1:
                local[...] = dot(neumann_own[:, 0:384], dual[0:384, :].astype(BF16))
        local[...] += dot(neumann_own[:, 384:768], dual[384:768, :].astype(BF16))
        for face in range(4):
            weighted_copies[face].wait_send()
        third_sum = jnp.sum(dual[...] * local[...], axis=0, keepdims=True)
        dots_out[...] = jnp.concatenate(
            [v[:, h : h + 128] for v in (third_sum, first_sum, second_sum) for h in (0, 128)]
            + [jnp.zeros((2, 128), F32)],
            axis=0,
        )
        all_dots[k, z] = dots_out[...]

        for device in planes:
            remote(dots_out, all_dots.at[k, z], dots_send, dots_recv.at[k], device).start()
        local_copies = send_faces(local, local_in, face_send, local_recv)

        @pl.when(k == 0)
        def _():
            block_copy(coarse, 2, after).wait()
            other = (region + 1 - 2 * core, coarse)
            copies = []
            for step in range(1, NX):
                i = lax.rem(coarse + step, NX)
                copies.append(
                    remote(
                        blocks.at[i, half], blocks.at[i, half], core_send.at[step - 1], core_recv.at[step - 1], other
                    )
                )
                copies[-1].start()
            for copy in copies:
                copy.wait()
            for i in range(NX):
                assembled[129 * i : 129 * (i + 1), 0:516] = blocks[i, 0:129, :]
            whole = assembled[...]
            inverse_high[...] = whole.astype(BF16)
            inverse_low[...] = (whole - rounded(whole)).astype(BF16)

        drain(all_loads.at[k, pl.ds(0, NZ - 1)], all_recv.at[k])
        part = [all_loads[k, i] for i in range(NZ)]
        tiles = []
        for t in range(5):
            tile = jnp.zeros((8, 128), F32)
            if t < 4:
                tile += jnp.where(lane < 124, pltpu.roll(part[4 * t], 124, 1), 0.0)
                tile += pltpu.roll(part[4 * t + 1], 28, 1) + pltpu.roll(part[4 * t + 2], 60, 1)
                tile += jnp.where(lane >= 64, pltpu.roll(part[4 * t + 3], 92, 1), 0.0)
            if t < 3:
                tile += jnp.where(lane >= 124, pltpu.roll(part[4 * t + 4], 124, 1), 0.0)
            if t > 0:
                tile += jnp.where(lane < 64, pltpu.roll(part[4 * t - 1], 92, 1), 0.0)
            tiles.append(tile)
        totals = jnp.concatenate(tiles, axis=1)
        high = rounded(totals)
        both = jnp.concatenate([high, totals - high], axis=0).astype(BF16)
        values = dot(both, inverse_high[...]) + dot(both, inverse_low[...])
        values = values[0:8] + values[8:16]
        energy = jnp.sum(totals * values, axis=1, keepdims=True)
        for t in range(5):
            shifted[t + 1] = values[:, 128 * t : 128 * (t + 1)]
        quarter, turn = lax.div(z, 4), lax.rem(z, 4)
        now, nearby, later = shifted[quarter], shifted[quarter + 1], shifted[quarter + 2]
        framed = jnp.where(
            turn == 0,
            jnp.where(lane < 4, pltpu.roll(now, 4, 1), pltpu.roll(nearby, 4, 1)),
            jnp.where(
                turn == 1,
                pltpu.roll(nearby, 100, 1),
                jnp.where(
                    turn == 2,
                    pltpu.roll(nearby, 68, 1),
                    jnp.where(lane < 36, pltpu.roll(nearby, 36, 1), pltpu.roll(later, 36, 1)),
                ),
            ),
        )
        framed = jnp.where(lane < USED, framed, jnp.where(lane == USED, energy, 0.0))

        drain(all_dots.at[k, pl.ds(0, NZ - 1)], dots_recv.at[k])
        back_out[0:8] = framed
        back_out[8:16] = jnp.sum(all_dots[k], axis=0)
        back_in[own] = back_out[...]

        for _, device in members:
            remote(back_out, back_in.at[own], back_send, back_recv, device).start()

        for face in range(4):
            local_copies[face].wait_send()
        for face in range(4):
            local_copies[face].wait_recv()
            local[rows(face), :] = difference(local[rows(face), :], local_in[rows(face), :], face)
        drain(back_in.at[pl.ds(0, GROUP - 1)], back_recv)
        coarse_values = back_in[:, 0:8, :].reshape(K, 128).T
        sums = jnp.sum(back_in[:, 8:16, :], axis=0)

        def joined(i):
            return jnp.concatenate([sums[i : i + 1], sums[i + 1 : i + 2]], axis=1)

        curve = 2.0 * (joined(0) + coarse_values[USED : USED + 1])
        product_sum = joined(2)
        ratio = jnp.where(k > 0, product_sum / scalars[0:1], 0.0)
        curve = curve + 2.0 * ratio * joined(4)
        curve = curve + jnp.where(k > 0, ratio * ratio * scalars[1:2], 0.0)
        step_len = product_sum / curve
        scalars[0:1] = product_sum
        scalars[1:2] = curve
        values_high = rounded(coarse_values[0:64])
        stacked = jnp.concatenate(
            [values_high, values_high, coarse_values[0:64] - values_high, jnp.zeros((64, K), F32)], axis=0
        ).astype(BF16)
        scalars[2:3] = ratio
        scalars[3:4] = step_len
        for face in range(4):
            at = rows(face)
            new_image = local[at, :] + dot(spread[at, :], stacked) + ratio * image[at, :]
            image[at, :] = new_image
            residual[at, :] -= step_len * new_image

        drain(loads_out.at[pl.ds(0, GROUP - 1)], group_send)
        drain(all_loads.at[k, pl.ds(0, NZ - 1)], plane_send)
        drain(all_dots.at[k, pl.ds(0, NZ - 1)], dots_send)
        drain(back_in.at[pl.ds(0, GROUP - 1)], back_send)
        return carry

    lax.fori_loop(0, ITERS, iteration, 0)
    update()


def restore(face_map, solved, residual, x_out, r_out, perms):
    one_hots(face_map, perms)
    for value, out in ((solved, x_out), (residual, r_out)):
        out[0, 0:128, :] = value[0:128, :]
        out[0, 384:512, :] = value[384:512, :]
        for i in range(2):
            out[0, WINDOWS[i], :] = permuted(perms[i].astype(F32).T.astype(BF16), value[WINDOWS[i], :])


def body(source, neumann, dirichlet, coupling, corner_map, face_map, coarse_inverse):
    field = pltpu.VMEM((M, K), F32)
    square = pltpu.VMEM((M, M), BF16)
    plain, dma, one = pltpu.SemaphoreType.REGULAR, pltpu.SemaphoreType.DMA, pltpu.SemaphoreType.DMA(())
    scratch = [
        pltpu.VMEM((1, 4, M), F32), pltpu.VMEM((1, 4), jnp.int32), pltpu.VMEM((1, 2, FACE), jnp.int32),
        pltpu.VMEM((129, 516), F32),
        field, field, field, field, field,
        field, field,
        pltpu.VMEM((4, FACE // 2, 128), F32), pltpu.VMEM((4, FACE // 2, 128), F32), pltpu.VMEM((M, 128), F32),
        pltpu.VMEM((2, 256, 256), BF16), pltpu.VMEM((M + 128, M), BF16), square, square, square,
        pltpu.VMEM((M, 256), BF16),
        pltpu.VMEM((NX, 144, 516), F32), pltpu.VMEM((WIDE, WIDE), F32),
        pltpu.VMEM((WIDE, WIDE), BF16), pltpu.VMEM((WIDE, WIDE), BF16),
        pltpu.VMEM((7, 8, 128), F32), pltpu.VMEM((8, K), F32),
        pltpu.VMEM((GROUP, 8, 128), F32), pltpu.VMEM((GROUP, 8, 128), F32),
        pltpu.VMEM((8, 128), F32), pltpu.VMEM((ITERS, NZ, 8, 128), F32),
        pltpu.VMEM((8, 128), F32), pltpu.VMEM((ITERS, NZ, 8, 128), F32),
        pltpu.VMEM((16, 128), F32), pltpu.VMEM((GROUP, 16, 128), F32),
        plain, plain, plain,
        dma((7,)), dma((4,)), dma((4,)), dma((4,)), dma((4,)), dma((4,)), dma((4,)),
        dma((3,)), dma((3,)), dma((3,)), dma((3,)),
        one, one, one, dma((ITERS,)), one, dma((ITERS,)), one, one,
    ]
    vmem, hbm = pl.BlockSpec(memory_space=pltpu.VMEM), pl.BlockSpec(memory_space=pl.ANY)
    solved, residual = pl.pallas_call(
        kernel,
        out_shape=(jax.ShapeDtypeStruct((M, K), F32), jax.ShapeDtypeStruct((M, K), F32)),
        in_specs=[hbm] * 7,
        out_specs=(vmem, vmem),
        scratch_shapes=scratch,
        compiler_params=pltpu.CompilerParams(collective_id=0, has_side_effects=True, vmem_limit_bytes=62 * 2**20),
        cost_estimate=pl.CostEstimate(flops=3 * 4 * M * M * K, bytes_accessed=6 * 10**6, transcendentals=0),
    )(source, neumann, dirichlet, coupling, corner_map, face_map, coarse_inverse)
    out = jax.ShapeDtypeStruct((1, M, K), F32)
    return pl.pallas_call(
        restore,
        out_shape=(out, out),
        in_specs=[vmem] * 3,
        out_specs=(vmem, vmem),
        scratch_shapes=[pltpu.VMEM((2, 256, 256), BF16)],
        compiler_params=pltpu.CompilerParams(vmem_limit_bytes=63 * 2**20),
    )(face_map, solved, residual)


def solution(mesh):
    split = P(("region", "coarse"), None, None)
    placed = (split, split, split, split, P(("region", "coarse"), None), split, P("coarse", None))
    return jax.shard_map(body, mesh=mesh, in_specs=placed, out_specs=(split, split), check_vma=False)
```

```python
import functools

import jax
import jax.numpy as jnp
from jax import lax
from jax.experimental import pallas as pl
from jax.experimental.pallas import tpu as pltpu
from jax.sharding import PartitionSpec as P

ITERS = 3
MESH = pl.DeviceIdType.MESH
F32, BF16 = jnp.float32, jnp.bfloat16

PLANE = 8
NX = 4
GROUP = PLANE * NX
NZ = 16
FACE = 192
M = 4 * FACE
K = 256
BASE = NX * PLANE
USED = NX * (PLANE + 3)
WIDE = 640
PACK = FACE // 8


def hops(step):
    return min(step, 4 - step)


MEMBERS = sorted(
    ((dy, dx, dc) for dy in range(4) for dx in range(4) for dc in range(2) if (dy, dx, dc) != (0, 0, 0)),
    key=lambda d: (-hops(d[0]) - hops(d[1]), d),
)
PLANES = sorted(range(1, NZ), key=lambda step: -min(step, NZ - step))


def rounded(value):
    return value.astype(BF16).astype(F32)


def dot(a, b):
    return jnp.dot(a, b, preferred_element_type=F32)


def dot_nt(a, b):
    return lax.dot_general(a, b, (((1,), (1,)), ((), ())), preferred_element_type=F32)


def permuted(onehot, value):
    high = value.astype(BF16)
    rest = value - high.astype(F32)
    middle = rest.astype(BF16)
    low = (rest - middle.astype(F32)).astype(BF16)
    return (dot(onehot, high) + dot(onehot, middle)) + dot(onehot, low)


WINDOWS = (pl.ds(128, 256), pl.ds(512, 256))


def one_hots(face_map, out):
    lanes = lax.broadcasted_iota(jnp.int32, (1, 64), 1)
    down = lax.broadcasted_iota(jnp.int32, (256, 256), 0)
    for i in range(2):
        target = jnp.concatenate([lanes, face_map[0, i : i + 1, :] + 64], axis=1)
        out[i] = (jnp.broadcast_to(target, (256, 256)) == down).astype(F32).astype(BF16)


def kernel(
    source, neumann, dirichlet, coupling_in, corner_map_in, face_map_in, coarse_inverse_in,
    solved, residual,
    coupling, corner_map, face_map, coarse_inverse, search, image, weighted, dual, local,
    weighted_in, local_in, corner_out, corner_in, frame,
    perms, dirichlet_all, neumann_own, raw_dirichlet, raw_neumann, spread,
    blocks, assembled, inverse_high, inverse_low, shifted, scalars,
    loads_out, loads_in, plane_loads, all_loads, dots_out, all_dots, back_out, back_in,
    line_sem, near_sem, far_sem, fetch_sem, face_send, source_recv, weighted_recv, local_recv, corner_send, corner_recv,
    block_send, block_recv, core_send, core_recv,
    group_send, loads_recv, plane_send, all_recv, dots_send, dots_recv, back_send, back_recv,
):
    region, coarse = lax.axis_index("region"), lax.axis_index("coarse")
    z, place = lax.div(region, PLANE), lax.rem(region, PLANE)
    core = lax.rem(region, 2)
    own = place * NX + coarse
    n_region = NZ * PLANE
    left = (lax.rem(region + n_region - 1, n_region), coarse)
    right = (lax.rem(region + 1, n_region), coarse)
    before = (region, lax.rem(coarse + NX - 1, NX))
    after = (region, lax.rem(coarse + 1, NX))
    neighbours = (left, right, before, after)
    partner_face = (1, 0, 3, 2)
    paired = (region > 0, region < n_region - 1, None, None)

    row = lax.div(place, 2)
    members = []
    for dy, dx, dc in MEMBERS:
        there = 2 * lax.rem(row + dy, 4) + (1 - core if dc else core)
        x = lax.rem(coarse + dx, NX)
        members.append((there * NX + x, (z * PLANE + there, x)))
    planes = [(lax.rem(z + step, NZ) * PLANE + place, coarse) for step in PLANES]

    def rows(face):
        return pl.ds(face * FACE, FACE)

    def remote(src, dst, send, recv, device):
        return pltpu.make_async_remote_copy(
            src_ref=src, dst_ref=dst, send_sem=send, recv_sem=recv, device_id=device, device_id_type=MESH
        )

    def drain(ref, sem):
        pltpu.make_async_copy(ref, ref, sem).wait()

    def send_faces(src, dst, send, recv):
        copies = [None] * 4
        for face in (2, 3, 0, 1):
            there = partner_face[face]
            copy = remote(
                src.at[rows(face)], dst.at[rows(there)], send.at[face], recv.at[there], neighbours[face]
            )
            copy.start()
            copies[there] = copy
        return copies

    def difference(mine, theirs, face):
        value = mine - theirs
        return value if paired[face] is None else jnp.where(paired[face], value, 0.0)

    line = [(region, lax.rem(coarse + dx, NX)) for dx in range(1, NX)]
    mates = [(z * PLANE + lax.rem(place + step, PLANE), coarse) for step in range(1, PLANE)]

    def plane_at(step):
        return (lax.rem(z + step + NZ, NZ) * PLANE + place, coarse)

    def greet(sem, devices):
        for device in devices:
            pl.semaphore_signal(sem, inc=1, device_id=device, device_id_type=MESH)

    barrier = pltpu.get_barrier_semaphore()
    first_round = [plane_at(2), plane_at(-2), plane_at(1), plane_at(-1), left, right] + line + mates
    greet(barrier, first_round)
    fetches = [
        pltpu.make_async_copy(src, dst, fetch_sem.at[i])
        for i, (src, dst) in enumerate(
            (
                (face_map_in, face_map),
                (corner_map_in, corner_map),
                (coupling_in, coupling),
                (source.at[0], dual),
                (dirichlet.at[0], raw_dirichlet),
                (neumann.at[0], raw_neumann),
                (coarse_inverse_in, coarse_inverse),
            )
        )
    ]
    for fetch in fetches:
        fetch.start()
    for fetch in fetches[0:3]:
        fetch.wait()

    one_hots(face_map, perms)

    across = lax.broadcasted_iota(jnp.int32, (128, M), 0)
    scattered = jnp.zeros((128, M), F32)
    for j in range(4):
        scattered += jnp.where(across == corner_map[0:1, j : j + 1] - BASE * z + NX, coupling[0, j : j + 1, :], 0.0)
    frame[...] = scattered.T
    for i in range(2):
        frame[WINDOWS[i], :] = permuted(perms[i], frame[WINDOWS[i], :])
    first_lane = NX * place + NX
    for face in range(4):
        value = pltpu.roll(frame[rows(face), :], 128 - first_lane, 1)
        corner_out[face] = sum(
            pltpu.roll(value[PACK * i : PACK * (i + 1)], 16 * i, 1) if i else value[0:PACK] for i in range(8)
        )

    fetches[3].wait()
    for i in range(2):
        dual[WINDOWS[i], :] = permuted(perms[i], dual[WINDOWS[i], :])

    pl.semaphore_wait(barrier, len(first_round))

    corners = [None] * 4
    for face in range(4):
        there = partner_face[face]
        copy = remote(
            corner_out.at[face], corner_in.at[there], corner_send.at[face], corner_recv.at[there], neighbours[face]
        )
        copy.start()
        corners[there] = copy
    faces = send_faces(dual, local_in, face_send, source_recv)
    greet(line_sem, line)
    greet(near_sem, [plane_at(2), plane_at(-2)])
    half = pl.ds(pl.multiple_of(core * 72, 8), 72)

    def block_copy(i, sem, device):
        return remote(blocks.at[i, half], blocks.at[i, half], block_send.at[sem], block_recv.at[sem], device)

    fetches[6].wait()
    blocks[coarse, 0:129, :] = coarse_inverse[...]
    blocks[coarse, 129:144, :] = jnp.zeros((15, 516), F32)
    block_copy(coarse, 0, after).start()
    block_copy(coarse, 1, before).start()
    assembled[...] = jnp.zeros((WIDE, WIDE), F32)
    solved[...] = jnp.zeros((M, K), F32)
    search[...] = jnp.zeros((M, K), F32)
    image[...] = jnp.zeros((M, K), F32)
    scalars[...] = jnp.ones((8, K), F32)
    shifted[...] = jnp.zeros((7, 8, 128), F32)

    def reorder(raw, out, first):
        for i in range(2):
            raw[WINDOWS[i], :] = dot(perms[i], raw[WINDOWS[i], :]).astype(BF16)
        out[pl.ds(first, M), 0:128] = raw[:, 0:128]
        out[pl.ds(first, M), 384:512] = raw[:, 384:512]
        for i in range(2):
            out[pl.ds(first, M), WINDOWS[i]] = dot_nt(raw[:, WINDOWS[i]], perms[i]).astype(BF16)

    fetches[4].wait()
    reorder(raw_dirichlet, dirichlet_all, 128)
    fetches[5].wait()
    reorder(raw_neumann, neumann_own, 0)
    pl.semaphore_wait(near_sem, 2)
    greet(far_sem, [plane_at(4), plane_at(-4)])

    in_use = lax.broadcasted_iota(jnp.int32, (PACK, 128), 1) < 8
    for face, shift in zip(range(4), (-NX, NX, 0, 0)):
        corners[face].wait_recv()
        packed = corner_in[face]
        theirs = jnp.concatenate(
            [jnp.where(in_use, pltpu.roll(packed, 128 - 16 * i, 1) if i else packed, 0.0) for i in range(8)], axis=0
        )
        theirs = pltpu.roll(theirs, first_lane + shift, 1)
        frame[rows(face), :] = difference(frame[rows(face), :], theirs, face)
    jumped = frame[...]
    high = rounded(jumped)
    low = jumped - high
    spread[...] = jnp.concatenate([high + pltpu.roll(low, 64, 1), high], axis=1).astype(BF16)
    jumped_t = jumped.T[0:64]
    high_t = rounded(jumped_t)
    product = dot(
        jnp.concatenate([high_t, jumped_t - high_t], axis=0).astype(BF16), dirichlet_all[pl.ds(128, M), :]
    )
    product = product[0:64] + product[64:128]
    high_t = rounded(product)
    dirichlet_all[0:128, :] = jnp.concatenate([high_t, product - high_t], axis=0).astype(BF16)
    for face in range(4):
        faces[face].wait_recv()
        residual[rows(face), :] = difference(dual[rows(face), :], local_in[rows(face), :], face)
    for face in range(4):
        faces[face].wait_send()
        corners[face].wait_send()

    pl.semaphore_wait(line_sem, NX - 1)
    lane = lax.broadcasted_iota(jnp.int32, (8, 128), 1)

    def update():
        for face in range(4):
            at = rows(face)
            new_search = dual[at, :] + scalars[2:3] * search[at, :]
            search[at, :] = new_search
            solved[at, :] += scalars[3:4] * new_search

    def iteration(k, carry):
        scaled = (0.5 * residual[...]).astype(BF16)
        load = dot(dirichlet_all[0:128, :], scaled)
        load = 0.5 * (load[0:64] + load[64:128])
        load = jnp.concatenate([load, jnp.zeros((64, K), F32)], axis=0)
        loads_out[...] = load.T.reshape(GROUP, 8, 128)
        loads_in[own] = loads_out[own]

        for peer, device in members:
            remote(loads_out.at[peer], loads_in.at[own], group_send, loads_recv, device).start()
        weighted[...] = dot(dirichlet_all[pl.ds(128, M), :], scaled)
        weighted_copies = send_faces(weighted, weighted_in, face_send, weighted_recv)

        @pl.when(k > 0)
        def _():
            update()

        @pl.when(k == 0)
        def _():
            for sem in range(2):
                block_copy(coarse, sem, after).wait()
            turn = 1 - 2 * core
            block_copy(lax.rem(coarse + NX - turn, NX), 2, (region, lax.rem(coarse + NX + turn, NX))).start()

        u = weighted[...]
        first_sum = jnp.sum(residual[...] * u, axis=0, keepdims=True)
        second_sum = jnp.sum(image[...] * u, axis=0, keepdims=True)

        @pl.when(k == 0)
        def _():
            pl.semaphore_wait(far_sem, 2)

        drain(loads_in.at[pl.ds(0, GROUP - 1)], loads_recv)
        plane_loads[...] = jnp.sum(loads_in[...], axis=0)
        all_loads[k, z] = plane_loads[...]

        for device in planes:
            remote(plane_loads, all_loads.at[k, z], plane_send, all_recv.at[k], device).start()

        for face in range(4):
            weighted_copies[face].wait_recv()
            dual[rows(face), :] = 0.5 * difference(weighted[rows(face), :], weighted_in[rows(face), :], face)
            if face == 1:
                local[...] = dot(neumann_own[:, 0:384], dual[0:384, :].astype(BF16))
        local[...] += dot(neumann_own[:, 384:768], dual[384:768, :].astype(BF16))
        for face in range(4):
            weighted_copies[face].wait_send()
        third_sum = jnp.sum(dual[...] * local[...], axis=0, keepdims=True)
        dots_out[...] = jnp.concatenate(
            [v[:, h : h + 128] for v in (third_sum, first_sum, second_sum) for h in (0, 128)]
            + [jnp.zeros((2, 128), F32)],
            axis=0,
        )
        all_dots[k, z] = dots_out[...]

        for device in planes:
            remote(dots_out, all_dots.at[k, z], dots_send, dots_recv.at[k], device).start()
        local_copies = send_faces(local, local_in, face_send, local_recv)

        @pl.when(k == 0)
        def _():
            block_copy(coarse, 2, after).wait()
            other = (region + 1 - 2 * core, coarse)
            copies = []
            for step in range(1, NX):
                i = lax.rem(coarse + step, NX)
                copies.append(
                    remote(
                        blocks.at[i, half], blocks.at[i, half], core_send.at[step - 1], core_recv.at[step - 1], other
                    )
                )
                copies[-1].start()
            for copy in copies:
                copy.wait()
            for i in range(NX):
                assembled[129 * i : 129 * (i + 1), 0:516] = blocks[i, 0:129, :]
            whole = assembled[...]
            inverse_high[...] = whole.astype(BF16)
            inverse_low[...] = (whole - rounded(whole)).astype(BF16)

        drain(all_loads.at[k, pl.ds(0, NZ - 1)], all_recv.at[k])
        part = [all_loads[k, i] for i in range(NZ)]
        tiles = []
        for t in range(5):
            tile = jnp.zeros((8, 128), F32)
            if t < 4:
                tile += jnp.where(lane < 124, pltpu.roll(part[4 * t], 124, 1), 0.0)
                tile += pltpu.roll(part[4 * t + 1], 28, 1) + pltpu.roll(part[4 * t + 2], 60, 1)
                tile += jnp.where(lane >= 64, pltpu.roll(part[4 * t + 3], 92, 1), 0.0)
            if t < 3:
                tile += jnp.where(lane >= 124, pltpu.roll(part[4 * t + 4], 124, 1), 0.0)
            if t > 0:
                tile += jnp.where(lane < 64, pltpu.roll(part[4 * t - 1], 92, 1), 0.0)
            tiles.append(tile)
        totals = jnp.concatenate(tiles, axis=1)
        high = rounded(totals)
        both = jnp.concatenate([high, totals - high], axis=0).astype(BF16)
        values = dot(both, inverse_high[...]) + dot(both, inverse_low[...])
        values = values[0:8] + values[8:16]
        energy = jnp.sum(totals * values, axis=1, keepdims=True)
        for t in range(5):
            shifted[t + 1] = values[:, 128 * t : 128 * (t + 1)]
        quarter, turn = lax.div(z, 4), lax.rem(z, 4)
        now, nearby, later = shifted[quarter], shifted[quarter + 1], shifted[quarter + 2]
        framed = jnp.where(
            turn == 0,
            jnp.where(lane < 4, pltpu.roll(now, 4, 1), pltpu.roll(nearby, 4, 1)),
            jnp.where(
                turn == 1,
                pltpu.roll(nearby, 100, 1),
                jnp.where(
                    turn == 2,
                    pltpu.roll(nearby, 68, 1),
                    jnp.where(lane < 36, pltpu.roll(nearby, 36, 1), pltpu.roll(later, 36, 1)),
                ),
            ),
        )
        framed = jnp.where(lane < USED, framed, jnp.where(lane == USED, energy, 0.0))

        drain(all_dots.at[k, pl.ds(0, NZ - 1)], dots_recv.at[k])
        back_out[0:8] = framed
        back_out[8:16] = jnp.sum(all_dots[k], axis=0)
        back_in[own] = back_out[...]

        for _, device in members:
            remote(back_out, back_in.at[own], back_send, back_recv, device).start()

        for face in range(4):
            local_copies[face].wait_send()
        for face in range(4):
            local_copies[face].wait_recv()
            local[rows(face), :] = difference(local[rows(face), :], local_in[rows(face), :], face)
        drain(back_in.at[pl.ds(0, GROUP - 1)], back_recv)
        coarse_values = back_in[:, 0:8, :].reshape(K, 128).T
        sums = jnp.sum(back_in[:, 8:16, :], axis=0)

        def joined(i):
            return jnp.concatenate([sums[i : i + 1], sums[i + 1 : i + 2]], axis=1)

        curve = 2.0 * (joined(0) + coarse_values[USED : USED + 1])
        product_sum = joined(2)
        ratio = jnp.where(k > 0, product_sum / scalars[0:1], 0.0)
        curve = curve + 2.0 * ratio * joined(4)
        curve = curve + jnp.where(k > 0, ratio * ratio * scalars[1:2], 0.0)
        step_len = product_sum / curve
        scalars[0:1] = product_sum
        scalars[1:2] = curve
        values_high = rounded(coarse_values[0:64])
        stacked = jnp.concatenate(
            [values_high, values_high, coarse_values[0:64] - values_high, jnp.zeros((64, K), F32)], axis=0
        ).astype(BF16)
        scalars[2:3] = ratio
        scalars[3:4] = step_len
        for face in range(4):
            at = rows(face)
            new_image = local[at, :] + dot(spread[at, :], stacked) + ratio * image[at, :]
            image[at, :] = new_image
            residual[at, :] -= step_len * new_image

        drain(loads_out.at[pl.ds(0, GROUP - 1)], group_send)
        drain(all_loads.at[k, pl.ds(0, NZ - 1)], plane_send)
        drain(all_dots.at[k, pl.ds(0, NZ - 1)], dots_send)
        drain(back_in.at[pl.ds(0, GROUP - 1)], back_send)
        return carry

    lax.fori_loop(0, ITERS, iteration, 0)
    update()


def restore(face_map, solved, residual, x_out, r_out, perms):
    one_hots(face_map, perms)
    for value, out in ((solved, x_out), (residual, r_out)):
        out[0, 0:128, :] = value[0:128, :]
        out[0, 384:512, :] = value[384:512, :]
        for i in range(2):
            out[0, WINDOWS[i], :] = permuted(perms[i].astype(F32).T.astype(BF16), value[WINDOWS[i], :])


def body(source, neumann, dirichlet, coupling, corner_map, face_map, coarse_inverse):
    field = pltpu.VMEM((M, K), F32)
    square = pltpu.VMEM((M, M), BF16)
    plain, dma, one = pltpu.SemaphoreType.REGULAR, pltpu.SemaphoreType.DMA, pltpu.SemaphoreType.DMA(())
    scratch = [
        pltpu.VMEM((1, 4, M), F32), pltpu.VMEM((1, 4), jnp.int32), pltpu.VMEM((1, 2, FACE), jnp.int32),
        pltpu.VMEM((129, 516), F32),
        field, field, field, field, field,
        field, field,
        pltpu.VMEM((4, PACK, 128), F32), pltpu.VMEM((4, PACK, 128), F32), pltpu.VMEM((M, 128), F32),
        pltpu.VMEM((2, 256, 256), BF16), pltpu.VMEM((M + 128, M), BF16), square, square, square,
        pltpu.VMEM((M, 256), BF16),
        pltpu.VMEM((NX, 144, 516), F32), pltpu.VMEM((WIDE, WIDE), F32),
        pltpu.VMEM((WIDE, WIDE), BF16), pltpu.VMEM((WIDE, WIDE), BF16),
        pltpu.VMEM((7, 8, 128), F32), pltpu.VMEM((8, K), F32),
        pltpu.VMEM((GROUP, 8, 128), F32), pltpu.VMEM((GROUP, 8, 128), F32),
        pltpu.VMEM((8, 128), F32), pltpu.VMEM((ITERS, NZ, 8, 128), F32),
        pltpu.VMEM((8, 128), F32), pltpu.VMEM((ITERS, NZ, 8, 128), F32),
        pltpu.VMEM((16, 128), F32), pltpu.VMEM((GROUP, 16, 128), F32),
        plain, plain, plain,
        dma((7,)), dma((4,)), dma((4,)), dma((4,)), dma((4,)), dma((4,)), dma((4,)),
        dma((3,)), dma((3,)), dma((3,)), dma((3,)),
        one, one, one, dma((ITERS,)), one, dma((ITERS,)), one, one,
    ]
    vmem, hbm = pl.BlockSpec(memory_space=pltpu.VMEM), pl.BlockSpec(memory_space=pl.ANY)
    solved, residual = pl.pallas_call(
        kernel,
        out_shape=(jax.ShapeDtypeStruct((M, K), F32), jax.ShapeDtypeStruct((M, K), F32)),
        in_specs=[hbm] * 7,
        out_specs=(vmem, vmem),
        scratch_shapes=scratch,
        compiler_params=pltpu.CompilerParams(collective_id=0, has_side_effects=True, vmem_limit_bytes=62 * 2**20),
        cost_estimate=pl.CostEstimate(flops=3 * 4 * M * M * K, bytes_accessed=6 * 10**6, transcendentals=0),
    )(source, neumann, dirichlet, coupling, corner_map, face_map, coarse_inverse)
    out = jax.ShapeDtypeStruct((1, M, K), F32)
    return pl.pallas_call(
        restore,
        out_shape=(out, out),
        in_specs=[vmem] * 3,
        out_specs=(vmem, vmem),
        scratch_shapes=[pltpu.VMEM((2, 256, 256), BF16)],
        compiler_params=pltpu.CompilerParams(vmem_limit_bytes=63 * 2**20),
    )(face_map, solved, residual)


def solution(mesh):
    split = P(("region", "coarse"), None, None)
    placed = (split, split, split, split, P(("region", "coarse"), None), split, P("coarse", None))
    return jax.shard_map(body, mesh=mesh, in_specs=placed, out_specs=(split, split), check_vma=False)
```

```python
import functools

import jax
import jax.numpy as jnp
from jax import lax
from jax.experimental import pallas as pl
from jax.experimental.pallas import tpu as pltpu
from jax.sharding import PartitionSpec as P

ITERS = 3
MESH = pl.DeviceIdType.MESH
F32, BF16 = jnp.float32, jnp.bfloat16

PLANE = 8
NX = 4
GROUP = PLANE * NX
NZ = 16
FACE = 192
M = 4 * FACE
K = 256
BASE = NX * PLANE
USED = NX * (PLANE + 3)
WIDE = 640
PACK = FACE // 8


def hops(step):
    return min(step, 4 - step)


MEMBERS = sorted(
    ((dy, dx, dc) for dy in range(4) for dx in range(4) for dc in range(2) if (dy, dx, dc) != (0, 0, 0)),
    key=lambda d: (-hops(d[0]) - hops(d[1]), d),
)
PLANES = sorted(range(1, NZ), key=lambda step: -min(step, NZ - step))


def rounded(value):
    return value.astype(BF16).astype(F32)


def dot(a, b):
    return jnp.dot(a, b, preferred_element_type=F32)


def dot_nt(a, b):
    return lax.dot_general(a, b, (((1,), (1,)), ((), ())), preferred_element_type=F32)


def permuted(onehot, value):
    high = value.astype(BF16)
    rest = value - high.astype(F32)
    middle = rest.astype(BF16)
    low = (rest - middle.astype(F32)).astype(BF16)
    return (dot(onehot, high) + dot(onehot, middle)) + dot(onehot, low)


WINDOWS = (pl.ds(128, 256), pl.ds(512, 256))


def one_hots(face_map, out):
    lanes = lax.broadcasted_iota(jnp.int32, (1, 64), 1)
    down = lax.broadcasted_iota(jnp.int32, (256, 256), 0)
    for i in range(2):
        target = jnp.concatenate([lanes, face_map[0, i : i + 1, :] + 64], axis=1)
        out[i] = (jnp.broadcast_to(target, (256, 256)) == down).astype(F32).astype(BF16)


def kernel(
    source, neumann, dirichlet, coupling_in, corner_map_in, face_map_in, coarse_inverse_in,
    solved_out, residual_out,
    solved, residual, coupling, corner_map, face_map, coarse_inverse, search, image, weighted, dual, local,
    weighted_in, local_in, corner_out, corner_in, frame,
    perms, dirichlet_all, neumann_own, raw_dirichlet, raw_neumann, spread,
    blocks, assembled, inverse_high, inverse_low, shifted, scalars,
    loads_out, loads_in, plane_loads, all_loads, dots_out, all_dots, back_out, back_in,
    line_sem, near_sem, far_sem, fetch_sem, face_send, source_recv, weighted_recv, local_recv, corner_send, corner_recv,
    block_send, block_recv, core_send, core_recv,
    group_send, loads_recv, plane_send, all_recv, dots_send, dots_recv, back_send, back_recv,
):
    region, coarse = lax.axis_index("region"), lax.axis_index("coarse")
    z, place = lax.div(region, PLANE), lax.rem(region, PLANE)
    core = lax.rem(region, 2)
    own = place * NX + coarse
    n_region = NZ * PLANE
    left = (lax.rem(region + n_region - 1, n_region), coarse)
    right = (lax.rem(region + 1, n_region), coarse)
    before = (region, lax.rem(coarse + NX - 1, NX))
    after = (region, lax.rem(coarse + 1, NX))
    neighbours = (left, right, before, after)
    partner_face = (1, 0, 3, 2)
    paired = (region > 0, region < n_region - 1, None, None)

    row = lax.div(place, 2)
    members = []
    for dy, dx, dc in MEMBERS:
        there = 2 * lax.rem(row + dy, 4) + (1 - core if dc else core)
        x = lax.rem(coarse + dx, NX)
        members.append((there * NX + x, (z * PLANE + there, x)))
    planes = [(lax.rem(z + step, NZ) * PLANE + place, coarse) for step in PLANES]

    def rows(face):
        return pl.ds(face * FACE, FACE)

    def remote(src, dst, send, recv, device):
        return pltpu.make_async_remote_copy(
            src_ref=src, dst_ref=dst, send_sem=send, recv_sem=recv, device_id=device, device_id_type=MESH
        )

    def drain(ref, sem):
        pltpu.make_async_copy(ref, ref, sem).wait()

    def send_faces(src, dst, send, recv):
        copies = [None] * 4
        for face in (2, 3, 0, 1):
            there = partner_face[face]
            copy = remote(
                src.at[rows(face)], dst.at[rows(there)], send.at[face], recv.at[there], neighbours[face]
            )
            copy.start()
            copies[there] = copy
        return copies

    def difference(mine, theirs, face):
        value = mine - theirs
        return value if paired[face] is None else jnp.where(paired[face], value, 0.0)

    line = [(region, lax.rem(coarse + dx, NX)) for dx in range(1, NX)]
    mates = [(z * PLANE + lax.rem(place + step, PLANE), coarse) for step in range(1, PLANE)]

    def plane_at(step):
        return (lax.rem(z + step + NZ, NZ) * PLANE + place, coarse)

    def greet(sem, devices):
        for device in devices:
            pl.semaphore_signal(sem, inc=1, device_id=device, device_id_type=MESH)

    barrier = pltpu.get_barrier_semaphore()
    first_round = [plane_at(2), plane_at(-2), plane_at(1), plane_at(-1), left, right] + line + mates
    greet(barrier, first_round)
    fetches = [
        pltpu.make_async_copy(src, dst, fetch_sem.at[i])
        for i, (src, dst) in enumerate(
            (
                (face_map_in, face_map),
                (corner_map_in, corner_map),
                (coupling_in, coupling),
                (source.at[0], dual),
                (dirichlet.at[0], raw_dirichlet),
                (neumann.at[0], raw_neumann),
                (coarse_inverse_in, coarse_inverse),
            )
        )
    ]
    for fetch in fetches:
        fetch.start()
    for fetch in fetches[0:3]:
        fetch.wait()

    one_hots(face_map, perms)

    across = lax.broadcasted_iota(jnp.int32, (128, M), 0)
    scattered = jnp.zeros((128, M), F32)
    for j in range(4):
        scattered += jnp.where(across == corner_map[0:1, j : j + 1] - BASE * z + NX, coupling[0, j : j + 1, :], 0.0)
    frame[...] = scattered.T
    for i in range(2):
        frame[WINDOWS[i], :] = permuted(perms[i], frame[WINDOWS[i], :])
    first_lane = NX * place + NX
    for face in range(4):
        value = pltpu.roll(frame[rows(face), :], 128 - first_lane, 1)
        corner_out[face] = sum(
            pltpu.roll(value[PACK * i : PACK * (i + 1)], 16 * i, 1) if i else value[0:PACK] for i in range(8)
        )

    fetches[3].wait()
    for i in range(2):
        dual[WINDOWS[i], :] = permuted(perms[i], dual[WINDOWS[i], :])

    pl.semaphore_wait(barrier, len(first_round))

    corners = [None] * 4
    for face in range(4):
        there = partner_face[face]
        copy = remote(
            corner_out.at[face], corner_in.at[there], corner_send.at[face], corner_recv.at[there], neighbours[face]
        )
        copy.start()
        corners[there] = copy
    faces = send_faces(dual, local_in, face_send, source_recv)
    greet(line_sem, line)
    greet(near_sem, [plane_at(2), plane_at(-2)])
    half = pl.ds(pl.multiple_of(core * 72, 8), 72)

    def block_copy(i, sem, device):
        return remote(blocks.at[i, half], blocks.at[i, half], block_send.at[sem], block_recv.at[sem], device)

    fetches[6].wait()
    blocks[coarse, 0:129, :] = coarse_inverse[...]
    blocks[coarse, 129:144, :] = jnp.zeros((15, 516), F32)
    block_copy(coarse, 0, after).start()
    block_copy(coarse, 1, before).start()
    assembled[...] = jnp.zeros((WIDE, WIDE), F32)
    solved[...] = jnp.zeros((M, K), F32)
    search[...] = jnp.zeros((M, K), F32)
    image[...] = jnp.zeros((M, K), F32)
    scalars[...] = jnp.ones((8, K), F32)
    shifted[...] = jnp.zeros((7, 8, 128), F32)

    def reorder(raw, out, first):
        for i in range(2):
            raw[WINDOWS[i], :] = dot(perms[i], raw[WINDOWS[i], :]).astype(BF16)
        out[pl.ds(first, M), 0:128] = raw[:, 0:128]
        out[pl.ds(first, M), 384:512] = raw[:, 384:512]
        for i in range(2):
            out[pl.ds(first, M), WINDOWS[i]] = dot_nt(raw[:, WINDOWS[i]], perms[i]).astype(BF16)

    fetches[4].wait()
    reorder(raw_dirichlet, dirichlet_all, 128)
    fetches[5].wait()
    reorder(raw_neumann, neumann_own, 0)
    pl.semaphore_wait(near_sem, 2)
    greet(far_sem, [plane_at(4), plane_at(-4)])

    in_use = lax.broadcasted_iota(jnp.int32, (PACK, 128), 1) < 8
    for face, shift in zip(range(4), (-NX, NX, 0, 0)):
        corners[face].wait_recv()
        packed = corner_in[face]
        theirs = jnp.concatenate(
            [jnp.where(in_use, pltpu.roll(packed, 128 - 16 * i, 1) if i else packed, 0.0) for i in range(8)], axis=0
        )
        theirs = pltpu.roll(theirs, first_lane + shift, 1)
        frame[rows(face), :] = difference(frame[rows(face), :], theirs, face)
    jumped = frame[...]
    high = rounded(jumped)
    low = jumped - high
    spread[...] = jnp.concatenate([high + pltpu.roll(low, 64, 1), high], axis=1).astype(BF16)
    jumped_t = jumped.T[0:64]
    high_t = rounded(jumped_t)
    product = dot(
        jnp.concatenate([high_t, jumped_t - high_t], axis=0).astype(BF16), dirichlet_all[pl.ds(128, M), :]
    )
    product = product[0:64] + product[64:128]
    high_t = rounded(product)
    dirichlet_all[0:128, :] = jnp.concatenate([high_t, product - high_t], axis=0).astype(BF16)
    for face in range(4):
        faces[face].wait_recv()
        residual[rows(face), :] = difference(dual[rows(face), :], local_in[rows(face), :], face)
    for face in range(4):
        faces[face].wait_send()
        corners[face].wait_send()

    pl.semaphore_wait(line_sem, NX - 1)
    lane = lax.broadcasted_iota(jnp.int32, (8, 128), 1)

    def update():
        for face in range(4):
            at = rows(face)
            new_search = dual[at, :] + scalars[2:3] * search[at, :]
            search[at, :] = new_search
            solved[at, :] += scalars[3:4] * new_search

    def iteration(k, carry):
        scaled = (0.5 * residual[...]).astype(BF16)
        load = dot(dirichlet_all[0:128, :], scaled)
        load = 0.5 * (load[0:64] + load[64:128])
        load = jnp.concatenate([load, jnp.zeros((64, K), F32)], axis=0)
        loads_out[...] = load.T.reshape(GROUP, 8, 128)
        loads_in[own] = loads_out[own]

        for peer, device in members:
            remote(loads_out.at[peer], loads_in.at[own], group_send, loads_recv, device).start()
        weighted[...] = dot(dirichlet_all[pl.ds(128, M), :], scaled)
        weighted_copies = send_faces(weighted, weighted_in, face_send, weighted_recv)

        @pl.when(k > 0)
        def _():
            update()

        @pl.when(k == 0)
        def _():
            for sem in range(2):
                block_copy(coarse, sem, after).wait()
            turn = 1 - 2 * core
            block_copy(lax.rem(coarse + NX - turn, NX), 2, (region, lax.rem(coarse + NX + turn, NX))).start()

        u = weighted[...]
        first_sum = jnp.sum(residual[...] * u, axis=0, keepdims=True)
        second_sum = jnp.sum(image[...] * u, axis=0, keepdims=True)

        @pl.when(k == 0)
        def _():
            pl.semaphore_wait(far_sem, 2)

        drain(loads_in.at[pl.ds(0, GROUP - 1)], loads_recv)
        plane_loads[...] = jnp.sum(loads_in[...], axis=0)
        all_loads[k, z] = plane_loads[...]

        for device in planes:
            remote(plane_loads, all_loads.at[k, z], plane_send, all_recv.at[k], device).start()

        for face in range(4):
            weighted_copies[face].wait_recv()
            dual[rows(face), :] = 0.5 * difference(weighted[rows(face), :], weighted_in[rows(face), :], face)
            if face == 1:
                local[...] = dot(neumann_own[:, 0:384], dual[0:384, :].astype(BF16))
        local[...] += dot(neumann_own[:, 384:768], dual[384:768, :].astype(BF16))
        for face in range(4):
            weighted_copies[face].wait_send()
        third_sum = jnp.sum(dual[...] * local[...], axis=0, keepdims=True)
        dots_out[...] = jnp.concatenate(
            [v[:, h : h + 128] for v in (third_sum, first_sum, second_sum) for h in (0, 128)]
            + [jnp.zeros((2, 128), F32)],
            axis=0,
        )
        all_dots[k, z] = dots_out[...]

        for device in planes:
            remote(dots_out, all_dots.at[k, z], dots_send, dots_recv.at[k], device).start()
        local_copies = send_faces(local, local_in, face_send, local_recv)

        @pl.when(k == 0)
        def _():
            block_copy(coarse, 2, after).wait()
            other = (region + 1 - 2 * core, coarse)
            copies = []
            for step in range(1, NX):
                i = lax.rem(coarse + step, NX)
                copies.append(
                    remote(
                        blocks.at[i, half], blocks.at[i, half], core_send.at[step - 1], core_recv.at[step - 1], other
                    )
                )
                copies[-1].start()
            for copy in copies:
                copy.wait()
            for i in range(NX):
                assembled[129 * i : 129 * (i + 1), 0:516] = blocks[i, 0:129, :]
            whole = assembled[...]
            inverse_high[...] = whole.astype(BF16)
            inverse_low[...] = (whole - rounded(whole)).astype(BF16)

        drain(all_loads.at[k, pl.ds(0, NZ - 1)], all_recv.at[k])
        part = [all_loads[k, i] for i in range(NZ)]
        tiles = []
        for t in range(5):
            tile = jnp.zeros((8, 128), F32)
            if t < 4:
                tile += jnp.where(lane < 124, pltpu.roll(part[4 * t], 124, 1), 0.0)
                tile += pltpu.roll(part[4 * t + 1], 28, 1) + pltpu.roll(part[4 * t + 2], 60, 1)
                tile += jnp.where(lane >= 64, pltpu.roll(part[4 * t + 3], 92, 1), 0.0)
            if t < 3:
                tile += jnp.where(lane >= 124, pltpu.roll(part[4 * t + 4], 124, 1), 0.0)
            if t > 0:
                tile += jnp.where(lane < 64, pltpu.roll(part[4 * t - 1], 92, 1), 0.0)
            tiles.append(tile)
        totals = jnp.concatenate(tiles, axis=1)
        high = rounded(totals)
        both = jnp.concatenate([high, totals - high], axis=0).astype(BF16)
        values = dot(both, inverse_high[...]) + dot(both, inverse_low[...])
        values = values[0:8] + values[8:16]
        energy = jnp.sum(totals * values, axis=1, keepdims=True)
        for t in range(5):
            shifted[t + 1] = values[:, 128 * t : 128 * (t + 1)]
        quarter, turn = lax.div(z, 4), lax.rem(z, 4)
        now, nearby, later = shifted[quarter], shifted[quarter + 1], shifted[quarter + 2]
        framed = jnp.where(
            turn == 0,
            jnp.where(lane < 4, pltpu.roll(now, 4, 1), pltpu.roll(nearby, 4, 1)),
            jnp.where(
                turn == 1,
                pltpu.roll(nearby, 100, 1),
                jnp.where(
                    turn == 2,
                    pltpu.roll(nearby, 68, 1),
                    jnp.where(lane < 36, pltpu.roll(nearby, 36, 1), pltpu.roll(later, 36, 1)),
                ),
            ),
        )
        framed = jnp.where(lane < USED, framed, jnp.where(lane == USED, energy, 0.0))

        drain(all_dots.at[k, pl.ds(0, NZ - 1)], dots_recv.at[k])
        back_out[0:8] = framed
        back_out[8:16] = jnp.sum(all_dots[k], axis=0)
        back_in[own] = back_out[...]

        for _, device in members:
            remote(back_out, back_in.at[own], back_send, back_recv, device).start()

        for face in range(4):
            local_copies[face].wait_send()
        for face in range(4):
            local_copies[face].wait_recv()
            local[rows(face), :] = difference(local[rows(face), :], local_in[rows(face), :], face)
        drain(back_in.at[pl.ds(0, GROUP - 1)], back_recv)
        coarse_values = back_in[:, 0:8, :].reshape(K, 128).T
        sums = jnp.sum(back_in[:, 8:16, :], axis=0)

        def joined(i):
            return jnp.concatenate([sums[i : i + 1], sums[i + 1 : i + 2]], axis=1)

        curve = 2.0 * (joined(0) + coarse_values[USED : USED + 1])
        product_sum = joined(2)
        ratio = jnp.where(k > 0, product_sum / scalars[0:1], 0.0)
        curve = curve + 2.0 * ratio * joined(4)
        curve = curve + jnp.where(k > 0, ratio * ratio * scalars[1:2], 0.0)
        step_len = product_sum / curve
        scalars[0:1] = product_sum
        scalars[1:2] = curve
        values_high = rounded(coarse_values[0:64])
        stacked = jnp.concatenate(
            [values_high, values_high, coarse_values[0:64] - values_high, jnp.zeros((64, K), F32)], axis=0
        ).astype(BF16)
        scalars[2:3] = ratio
        scalars[3:4] = step_len
        for face in range(4):
            at = rows(face)
            new_image = local[at, :] + dot(spread[at, :], stacked) + ratio * image[at, :]
            image[at, :] = new_image
            residual[at, :] -= step_len * new_image

        drain(loads_out.at[pl.ds(0, GROUP - 1)], group_send)
        drain(all_loads.at[k, pl.ds(0, NZ - 1)], plane_send)
        drain(all_dots.at[k, pl.ds(0, NZ - 1)], dots_send)
        drain(back_in.at[pl.ds(0, GROUP - 1)], back_send)
        return carry

    lax.fori_loop(0, ITERS, iteration, 0)
    results = [
        pltpu.make_async_copy(residual, residual_out, fetch_sem.at[7]),
        pltpu.make_async_copy(solved, solved_out, fetch_sem.at[8]),
    ]
    results[0].start()
    update()
    results[1].start()
    for result in results:
        result.wait()


def restore(face_map, solved, residual, x_out, r_out, perms):
    one_hots(face_map, perms)
    for value, out in ((solved, x_out), (residual, r_out)):
        out[0, 0:128, :] = value[0:128, :]
        out[0, 384:512, :] = value[384:512, :]
        for i in range(2):
            out[0, WINDOWS[i], :] = permuted(perms[i].astype(F32).T.astype(BF16), value[WINDOWS[i], :])


def body(source, neumann, dirichlet, coupling, corner_map, face_map, coarse_inverse):
    field = pltpu.VMEM((M, K), F32)
    square = pltpu.VMEM((M, M), BF16)
    plain, dma, one = pltpu.SemaphoreType.REGULAR, pltpu.SemaphoreType.DMA, pltpu.SemaphoreType.DMA(())
    scratch = [
        field, field, pltpu.VMEM((1, 4, M), F32), pltpu.VMEM((1, 4), jnp.int32), pltpu.VMEM((1, 2, FACE), jnp.int32),
        pltpu.VMEM((129, 516), F32),
        field, field, field, field, field,
        field, field,
        pltpu.VMEM((4, PACK, 128), F32), pltpu.VMEM((4, PACK, 128), F32), pltpu.VMEM((M, 128), F32),
        pltpu.VMEM((2, 256, 256), BF16), pltpu.VMEM((M + 128, M), BF16), square, square, square,
        pltpu.VMEM((M, 256), BF16),
        pltpu.VMEM((NX, 144, 516), F32), pltpu.VMEM((WIDE, WIDE), F32),
        pltpu.VMEM((WIDE, WIDE), BF16), pltpu.VMEM((WIDE, WIDE), BF16),
        pltpu.VMEM((7, 8, 128), F32), pltpu.VMEM((8, K), F32),
        pltpu.VMEM((GROUP, 8, 128), F32), pltpu.VMEM((GROUP, 8, 128), F32),
        pltpu.VMEM((8, 128), F32), pltpu.VMEM((ITERS, NZ, 8, 128), F32),
        pltpu.VMEM((8, 128), F32), pltpu.VMEM((ITERS, NZ, 8, 128), F32),
        pltpu.VMEM((16, 128), F32), pltpu.VMEM((GROUP, 16, 128), F32),
        plain, plain, plain,
        dma((9,)), dma((4,)), dma((4,)), dma((4,)), dma((4,)), dma((4,)), dma((4,)),
        dma((3,)), dma((3,)), dma((3,)), dma((3,)),
        one, one, one, dma((ITERS,)), one, dma((ITERS,)), one, one,
    ]
    vmem, hbm = pl.BlockSpec(memory_space=pltpu.VMEM), pl.BlockSpec(memory_space=pl.ANY)
    solved, residual = pl.pallas_call(
        kernel,
        out_shape=(jax.ShapeDtypeStruct((M, K), F32), jax.ShapeDtypeStruct((M, K), F32)),
        in_specs=[hbm] * 7,
        out_specs=(hbm, hbm),
        scratch_shapes=scratch,
        compiler_params=pltpu.CompilerParams(collective_id=0, has_side_effects=True, vmem_limit_bytes=62 * 2**20),
        cost_estimate=pl.CostEstimate(flops=3 * 4 * M * M * K, bytes_accessed=6 * 10**6, transcendentals=0),
    )(source, neumann, dirichlet, coupling, corner_map, face_map, coarse_inverse)
    out = jax.ShapeDtypeStruct((1, M, K), F32)
    return pl.pallas_call(
        restore,
        out_shape=(out, out),
        in_specs=[vmem] * 3,
        out_specs=(vmem, vmem),
        scratch_shapes=[pltpu.VMEM((2, 256, 256), BF16)],
        compiler_params=pltpu.CompilerParams(vmem_limit_bytes=63 * 2**20),
    )(face_map, solved, residual)


def solution(mesh):
    split = P(("region", "coarse"), None, None)
    placed = (split, split, split, split, P(("region", "coarse"), None), split, P("coarse", None))
    return jax.shard_map(body, mesh=mesh, in_specs=placed, out_specs=(split, split), check_vma=False)
```
